32 devices in a mesh: context: 4 (over z), head: 8 (over y, x, core).
Axes of the slice: x: 2, y: 2, z: 4, core: 2. Of those that a mesh axis runs over, the one named last changes fastest.
Arguments:
- x_in: bfloat16 [4096, 2048], P('context', 'head'), may hold values from -6 to 6
- bc_in: bfloat16 [4096, 4096], P('context'), may hold values from -6 to 6
- z_in: bfloat16 [4096, 2048], P('context', 'head'), may hold values from -6 to 6
- dt_in: bfloat16 [32, 4096], P('head', 'context'), may hold values from -4 to 4
- conv_x_w: float32 [4, 2048], P(None, 'head'), may hold values from -3 to 3
- conv_x_b: float32 [2048], P('head'), may hold values from -1.5 to 1.5
- conv_bc_w: float32 [4, 4096], replicated, may hold values from -3 to 3
- conv_bc_b: float32 [4096], replicated, may hold values from -1.5 to 1.5
- dt_bias: float32 [32], P('head'), may hold values from -3.5 to -2.5
- a_log: float32 [32], P('head'), may hold values from -12 to 0
- skip_gain: float32 [32], P('head'), may hold values from 1 to 4
- norm_w: float32 [2048], P('head'), may hold values from 0.5 to 1.5
- doc_len: int32 [16], replicated, may hold values from 1 to 2048, 4096 in all
Outputs:
- ssd_out: bfloat16 [4096, 2048], P('context', 'head')
The draws below stay inside these ranges and needn't reach their ends.
Inputs may be any that keep to these rules, and one draw needn't show every extreme that they name: `doc_len`: the lengths sum to 4096; the longest is exactly 2048.
All inputs are finite; a program needn't handle non-finite values.
Results may differ from the reference program's by a relative error of at most 0.0034.
Values may be sent and summed in bfloat16 or wider, within the bound.
A program may use at most 64 MiB of HBM per device.

```python
import math
import jax
import jax.numpy as jnp
import numpy as np
from jax import lax

HEAD_DIM = 64
STATE = 256
GROUPS = 8
CONV = 4
BLOCK = 256
HEADS = 32
TOKENS = 4096
DOCS = 16


def draw_a_log(key, part):
    pick_key, fast_key, slow_key = jax.random.split(key, 3)
    slow_share = 0.5
    slow_head = jax.random.bernoulli(pick_key, slow_share, (HEADS,))
    fast_log = jax.random.uniform(fast_key, (HEADS,), jnp.float32, jnp.log(0.3), 0.0)
    slow_log = jnp.log(40.0 / TOKENS) + jax.random.uniform(slow_key, (HEADS,), jnp.float32, jnp.log(0.05), jnp.log(2.0))
    return jnp.where(slow_head, slow_log, fast_log).astype(jnp.float32)


def level_of(rng, extent, pieces, smallest, high):
    gain = 1.0
    for position, blocks in pieces:
        steps = jax.random.uniform(jax.random.fold_in(jax.random.fold_in(rng, 6), position), (blocks,), jnp.float32, smallest / len(pieces), high / len(pieces))
        gain = gain * jnp.repeat(jnp.exp(steps), extent[position] // blocks).reshape((-1,) + (1,) * (len(extent) - 1 - position))
    return gain


def profile(number_of, total, reach, skew):
    loads = [(1 << 20) // math.isqrt(rank ** skew) + 1 for rank in range(2, number_of + 1)]
    spare, holding = total - reach - (number_of - 1), [1] * (number_of - 1)
    while spare > 0:
        movable = [i for i in range(number_of - 1) if holding[i] < reach]
        mass, left = sum([loads[i] for i in movable]), spare
        for i in movable:
            more = min(reach - holding[i], max(1, left * loads[i] // mass), spare)
            holding[i] = holding[i] + more
            spare = spare - more
    return np.array([reach] + holding)


def ragged_sizes(rng, number_of, total, bound, skew):
    if number_of == 2:
        one = jax.random.randint(rng, (), max(1, total - bound), min(bound, total - 1) + 1)
        return jnp.stack([one, total - one])
    tallies = jnp.asarray(profile(number_of, total, bound, skew), jnp.int32)
    twos = (number_of - 1) // 2
    source_of, receiver = tallies[1:1 + 2 * twos:2], tallies[2:2 + 2 * twos:2]
    room = jnp.minimum(source_of - 1, bound - receiver)
    shifted = jax.random.randint(jax.random.fold_in(rng, 1), (twos,), 0, 1 << 20) % (room + 1)
    tallies = tallies.at[1:1 + 2 * twos:2].set(source_of - shifted).at[2:2 + 2 * twos:2].set(receiver + shifted)
    return tallies[jax.random.permutation(jax.random.fold_in(rng, 2), number_of)]


def gaussian(own_key, dims, width, bound, pieces=(), kind=jnp.bfloat16):
    array = width * jax.random.normal(own_key, dims, jnp.float32)
    if pieces:
        array = array * level_of(own_key, dims, pieces, -0.22, 0.18)
    return jnp.clip(array, -bound, bound).astype(kind)


def setup_inputs(seed: int = 0) -> dict:
    seeds = jax.random.split(jax.random.key(seed), 14)
    x_in = gaussian(seeds[0], (TOKENS, HEADS * HEAD_DIM), 1.0, 6.0, ((0, 4), (1, 8)))
    bc_in = gaussian(seeds[1], (TOKENS, 2 * GROUPS * STATE), 1.0, 6.0, ((0, 4),))
    z_in = gaussian(seeds[2], (TOKENS, HEADS * HEAD_DIM), 1.0, 6.0, ((0, 4), (1, 8)))
    dt_in = gaussian(seeds[3], (HEADS, TOKENS), 1.0, 4.0, ((0, 8), (1, 4)))
    conv_x_w = gaussian(seeds[4], (CONV, HEADS * HEAD_DIM), CONV ** -0.5, 3.0, ((1, 8),), jnp.float32)
    conv_x_b = gaussian(seeds[5], (HEADS * HEAD_DIM,), 0.3, 1.5, ((0, 8),), jnp.float32)
    conv_bc_w = gaussian(seeds[6], (CONV, 2 * GROUPS * STATE), CONV ** -0.5, 3.0, (), jnp.float32)
    conv_bc_b = gaussian(seeds[7], (2 * GROUPS * STATE,), 0.3, 1.5, (), jnp.float32)
    dt_bias = jnp.clip(-3.5 + 1.0 * jax.random.uniform(seeds[8], (HEADS,), jnp.float32) ** level_of(seeds[8], (HEADS,), ((0, 8),), -0.2, 0.2), -3.5, -2.5)
    a_log = draw_a_log(jax.random.fold_in(seeds[13], 71), 0)
    skip_gain = jnp.clip(1.0 + 3.0 * jax.random.uniform(seeds[10], (HEADS,), jnp.float32) ** level_of(seeds[10], (HEADS,), ((0, 8),), -0.2, 0.2), 1.0, 4.0)
    norm_w = jnp.clip(1.0 + 0.1 * jax.random.normal(seeds[11], (HEADS * HEAD_DIM,), jnp.float32), 0.5, 1.5)
    doc_len = ragged_sizes(seeds[12], DOCS, TOKENS, TOKENS // 2, 2).astype(jnp.int32)
    return dict(x_in=x_in, bc_in=bc_in, z_in=z_in, dt_in=dt_in, conv_x_w=conv_x_w, conv_x_b=conv_x_b, conv_bc_w=conv_bc_w, conv_bc_b=conv_bc_b, dt_bias=dt_bias, a_log=a_log, skip_gain=skip_gain, norm_w=norm_w, doc_len=doc_len)


exact_mode = lax.Precision.HIGHEST
norm_floor = 1e-05

def doc_marks(doc_len, positions):
    doc_ends = jnp.cumsum(doc_len).astype(jnp.int32)
    begins = doc_ends - doc_len
    segment = lax.optimization_barrier(jnp.sum((doc_ends[None, :] <= positions[:, None]).astype(jnp.int32), axis=1))
    opening = lax.optimization_barrier(jnp.sum((begins[None, :] == positions[:, None]).astype(jnp.int32), axis=1))
    return (segment, opening)

def conv_silu(extended, segment_ext, weights, biases, rows_count):
    newest = segment_ext[CONV - 1:CONV - 1 + rows_count]
    summed = jnp.zeros((rows_count, extended.shape[1]), jnp.float32) + biases[None, :]
    for offset in range(CONV):
        same_doc = (segment_ext[offset:offset + rows_count] == newest).astype(jnp.float32)
        summed = summed + weights[offset][None, :] * extended[offset:offset + rows_count].astype(jnp.float32) * same_doc[:, None]
    return jax.nn.silu(summed).astype(jnp.bfloat16)

def reference(x_in, bc_in, z_in, dt_in, conv_x_w, conv_x_b, conv_bc_w, conv_bc_b, dt_bias, a_log, skip_gain, norm_w, doc_len):
    rows_all = x_in.shape[0]
    per_group = HEADS // GROUPS
    group_width = per_group * HEAD_DIM
    positions = jnp.arange(rows_all, dtype=jnp.int32)
    segment, opening = doc_marks(doc_len, positions)
    segment_ext = jnp.concatenate([jnp.zeros((CONV - 1,), jnp.int32), segment])
    blocks = rows_all // BLOCK
    seg_blocks = segment.reshape(blocks, BLOCK)
    alive_mask = jnp.cumsum(opening.reshape(blocks, BLOCK), axis=1) == 0
    lower_tri = jnp.arange(BLOCK)[:, None] >= jnp.arange(BLOCK)[None, :]
    same_block = (seg_blocks[:, :, None] == seg_blocks[:, None, :]) & lower_tri[None]
    tail_same = seg_blocks == seg_blocks[:, -1:]

    def one_group(group_index):
        x_part = lax.dynamic_slice_in_dim(x_in, group_index * group_width, group_width, 1)
        b_part = lax.dynamic_slice_in_dim(bc_in, group_index * STATE, STATE, 1)
        c_part = lax.dynamic_slice_in_dim(bc_in, (GROUPS + group_index) * STATE, STATE, 1)
        raw_rows = jnp.concatenate([x_part, b_part, c_part], axis=1)
        extended = jnp.concatenate([jnp.zeros((CONV - 1, raw_rows.shape[1]), jnp.bfloat16), raw_rows], axis=0)
        weights = jnp.concatenate([lax.dynamic_slice_in_dim(conv_x_w, group_index * group_width, group_width, 1), lax.dynamic_slice_in_dim(conv_bc_w, group_index * STATE, STATE, 1), lax.dynamic_slice_in_dim(conv_bc_w, (GROUPS + group_index) * STATE, STATE, 1)], axis=1)
        biases = jnp.concatenate([lax.dynamic_slice_in_dim(conv_x_b, group_index * group_width, group_width, 0), lax.dynamic_slice_in_dim(conv_bc_b, group_index * STATE, STATE, 0), lax.dynamic_slice_in_dim(conv_bc_b, (GROUPS + group_index) * STATE, STATE, 0)], axis=0)
        mixed = conv_silu(extended, segment_ext, weights, biases, rows_all)
        b_vals = mixed[:, group_width:group_width + STATE].astype(jnp.float32).reshape(blocks, BLOCK, STATE)
        c_vals = mixed[:, group_width + STATE:].astype(jnp.float32).reshape(blocks, BLOCK, STATE)
        inner_prod = jnp.einsum('ctn,csn->cts', c_vals, b_vals, precision=exact_mode)

        def one_head(local_head):
            head_global = group_index * per_group + local_head
            x_head = lax.dynamic_slice_in_dim(mixed, local_head * HEAD_DIM, HEAD_DIM, 1).astype(jnp.float32)
            dt_row = lax.dynamic_index_in_dim(dt_in, head_global, 0, keepdims=False).astype(jnp.float32)
            step_size = jax.nn.softplus(dt_row + dt_bias[head_global])
            rate_value = -jnp.exp(a_log[head_global])
            weighted = (x_head * step_size[:, None]).reshape(blocks, BLOCK, HEAD_DIM)
            running = jnp.cumsum((step_size * rate_value).reshape(blocks, BLOCK), axis=1)
            gap_logs = jnp.minimum(running[:, :, None] - running[:, None, :], 0.0)
            mixing = jnp.where(same_block, jnp.exp(gap_logs), 0.0) * inner_prod
            intra_out = jnp.einsum('cts,csp->ctp', mixing, weighted, precision=exact_mode)
            tail_weight = jnp.where(tail_same, jnp.exp(running[:, -1:] - running), 0.0)
            summaries = jnp.einsum('csp,csn->cpn', weighted * tail_weight[:, :, None], b_vals, precision=exact_mode)
            carry_decay = jnp.exp(running[:, -1]) * alive_mask[:, -1].astype(jnp.float32)

            def advance(state_now, inputs):
                summary, factor = inputs
                return (factor * state_now + summary, state_now)
            _, incoming = lax.scan(advance, jnp.zeros((HEAD_DIM, STATE), jnp.float32), (summaries, carry_decay))
            entry_scale = alive_mask.astype(jnp.float32) * jnp.exp(running)
            from_state = jnp.einsum('ctn,cpn->ctp', c_vals, incoming, precision=exact_mode) * entry_scale[:, :, None]
            return (intra_out + from_state).reshape(rows_all, HEAD_DIM) + skip_gain[head_global] * x_head
        per_head = lax.map(one_head, jnp.arange(per_group, dtype=jnp.int32))
        outputs = jnp.transpose(per_head, (1, 0, 2)).reshape(rows_all, group_width)
        z_part = lax.dynamic_slice_in_dim(z_in, group_index * group_width, group_width, 1).astype(jnp.float32)
        return outputs * jax.nn.silu(z_part)
    group_outs = lax.map(one_group, jnp.arange(GROUPS, dtype=jnp.int32))
    square_sum = lax.optimization_barrier(jnp.sum(lax.optimization_barrier(jnp.sum(group_outs * group_outs, axis=2)), axis=0))
    scale_rows = lax.rsqrt(square_sum / (HEADS * HEAD_DIM) + norm_floor)
    gated_all = jnp.transpose(group_outs, (1, 0, 2)).reshape(rows_all, HEADS * HEAD_DIM)
    return (gated_all * scale_rows[:, None] * norm_w[None, :]).astype(jnp.bfloat16)
```

```python
import functools
import math

import jax
import jax.numpy as jnp
from jax import lax
from jax.experimental import pallas as pl
from jax.experimental.pallas import tpu as pltpu
from jax.sharding import PartitionSpec as P

HEAD_DIM = 64
STATE = 256
GROUPS = 8
CONV = 4
BLOCK = 256
TILE = 128
HALO = 16
CHUNKS = 4
LOG2E = math.log2(math.e)
NORM_FLOOR = 1e-05
F32 = jnp.float32
BF16 = jnp.bfloat16


def dot(a, b, dims):
    return lax.dot_general(a, b, (dims, ((), ())), preferred_element_type=F32)


def silu_half(h):
    return h + h * jnp.tanh(h)


def split_rows(v, parts):
    pieces = []
    for _ in range(parts):
        piece = v.astype(BF16).astype(F32)
        pieces.append(piece)
        v = v - piece
    return jnp.concatenate(pieces, axis=0).astype(BF16)


def layer_kernel(
    n_ctx,
    n_head,
    x_hbm,
    bc_hbm,
    z_hbm,
    dt_ref,
    xw_ref,
    xb_ref,
    bcw_ref,
    bcb_ref,
    dt_bias,
    a_log,
    skip_gain,
    nw_ref,
    doc_len,
    out_hbm,
    ext,
    z_buf,
    mixed,
    tail_buf,
    entry_buf,
    state_buf,
    end_buf,
    y_buf,
    gate_buf,
    send_buf,
    recv_buf,
    sums,
    out_buf,
    load_sems,
    halo_send,
    halo_recv,
    state_send,
    state_recv,
    sums_send,
    sums_recv,
    out_sems,
):
    rows = x_hbm.shape[0]
    width = x_hbm.shape[1]
    heads = dt_ref.shape[0]
    docs = doc_len.shape[0]
    blocks = rows // BLOCK
    tiles = rows // TILE
    ctx = lax.axis_index("context")
    me = lax.axis_index("head")
    per_group = n_head * heads // GROUPS
    group = me * heads // per_group
    b_at = pl.multiple_of(group * STATE, STATE)
    c_at = pl.multiple_of((GROUPS + group) * STATE, STATE)
    not_last = ctx < n_ctx - 1

    barrier = pltpu.get_barrier_semaphore()

    @pl.when(ctx > 0)
    def _():
        pl.semaphore_signal(
            barrier, inc=1, device_id=(ctx - 1, me), device_id_type=pl.DeviceIdType.MESH
        )

    peers = [lax.rem(me + d, n_head) for d in range(1, n_head)]
    for peer in peers:
        pl.semaphore_signal(
            barrier, inc=1, device_id=(ctx, peer), device_id_type=pl.DeviceIdType.MESH
        )

    own = pl.ds(HALO, rows)
    loads = [
        pltpu.make_async_copy(x_hbm, ext.at[own, pl.ds(0, width)], load_sems.at[0]),
        pltpu.make_async_copy(
            bc_hbm.at[:, pl.ds(b_at, STATE)], ext.at[own, pl.ds(width, STATE)], load_sems.at[1]
        ),
        pltpu.make_async_copy(
            bc_hbm.at[:, pl.ds(c_at, STATE)],
            ext.at[own, pl.ds(width + STATE, STATE)],
            load_sems.at[2],
        ),
        pltpu.make_async_copy(z_hbm, z_buf, load_sems.at[3]),
    ]
    for load in loads:
        load.start()

    @pl.when(ctx == 0)
    def _():
        ext[pl.ds(0, HALO), :] = jnp.zeros((HALO, width + 2 * STATE), BF16)
        recv_buf[...] = jnp.zeros((STATE, width), BF16)

    pl.semaphore_wait(barrier, n_head - 1 + jnp.where(not_last, 1, 0))

    right = (jnp.minimum(ctx + 1, n_ctx - 1), me)
    last_rows = pl.ds(rows - HALO, HALO)
    halo_src = [
        x_hbm.at[last_rows, :],
        bc_hbm.at[last_rows, pl.ds(b_at, STATE)],
        bc_hbm.at[last_rows, pl.ds(c_at, STATE)],
    ]
    halo_at = [pl.ds(0, width), pl.ds(width, STATE), pl.ds(width + STATE, STATE)]

    def halo_copy(i):
        return pltpu.make_async_remote_copy(
            src_ref=halo_src[i],
            dst_ref=ext.at[pl.ds(0, HALO), halo_at[i]],
            send_sem=halo_send.at[i],
            recv_sem=halo_recv.at[i],
            device_id=right,
            device_id_type=pl.DeviceIdType.MESH,
        )

    @pl.when(not_last)
    def _():
        for i in range(3):
            halo_copy(i).start()

    first = ctx * rows
    ends, begins, total = [], [], jnp.int32(0)
    for d in range(docs):
        begins.append(total)
        total = total + doc_len[d]
        ends.append(total)

    def tokens_left(pos):
        end = jnp.zeros_like(pos)
        for d in reversed(range(docs)):
            end = jnp.where(pos < ends[d], ends[d], end)
        return jnp.where(pos < 0, -1, end - 1 - pos)

    ext_lanes = rows + TILE
    left_ext = tokens_left(first - HALO + lax.broadcasted_iota(jnp.int32, (1, ext_lanes), 1))
    lane = lax.broadcasted_iota(jnp.int32, (1, rows), 1)
    pos = first + lane
    left = tokens_left(pos)
    begin = jnp.zeros_like(pos)
    for d in range(docs):
        begin = jnp.where(pos >= begins[d], begins[d], begin)
    lane_b = lax.rem(lane, BLOCK)
    alive = pos - begin > lane_b
    tail_same = left >= BLOCK - 1 - lane_b

    head_row = lax.broadcasted_iota(jnp.int32, (heads, rows), 0)
    bias_col = jnp.zeros((heads, rows), F32)
    alog_col = jnp.zeros((heads, rows), F32)
    for h in range(heads):
        bias_col = jnp.where(head_row == h, dt_bias[h], bias_col)
        alog_col = jnp.where(head_row == h, a_log[h], alog_col)
    raw = dt_ref[...].astype(F32) + bias_col
    step = jnp.maximum(raw, 0.0) + jnp.log1p(jnp.exp(-jnp.abs(raw)))
    log_decay = step * (jnp.exp(alog_col) * (-LOG2E))
    per_block = jnp.concatenate(
        [log_decay[:, c * BLOCK : (c + 1) * BLOCK] for c in range(blocks)], axis=0
    )
    upper = (
        lax.broadcasted_iota(jnp.int32, (BLOCK, BLOCK), 0)
        <= lax.broadcasted_iota(jnp.int32, (BLOCK, BLOCK), 1)
    )
    n_run = blocks * heads
    summed = dot(split_rows(per_block, 3), upper.astype(F32).astype(BF16), ((1,), (0,)))
    run = summed[:n_run] + summed[n_run : 2 * n_run] + summed[2 * n_run :]
    run_col = jnp.transpose(run)
    ends_run = run[:, BLOCK - 1 : BLOCK]
    running = jnp.concatenate([run[c * heads : (c + 1) * heads] for c in range(blocks)], axis=1)
    to_end = jnp.concatenate(
        [
            ends_run[c * heads : (c + 1) * heads] - run[c * heads : (c + 1) * heads]
            for c in range(blocks)
        ],
        axis=1,
    )
    tail_rows = jnp.where(tail_same, jnp.exp2(to_end), 0.0) * step
    entry_rows = jnp.where(alive, jnp.exp2(running), 0.0)

    spread = (
        lax.broadcasted_iota(jnp.int32, (heads, width), 0)
        == lax.broadcasted_iota(jnp.int32, (heads, width), 1) // HEAD_DIM
    ).astype(F32)
    spread2 = jnp.concatenate([spread, spread], axis=0).astype(BF16)
    tail_buf[...] = dot(split_rows(tail_rows, 2), spread2, ((0,), (0,)))
    entry_buf[...] = dot(split_rows(entry_rows, 2), spread2, ((0,), (0,)))

    decay_rows = []
    for c in range(blocks):
        at = c * BLOCK + BLOCK - 1
        decay_rows.append(jnp.sum(entry_rows[:, at : at + 1] * spread, axis=0, keepdims=True))
    skip_row = jnp.zeros((1, width), F32)
    head_lane = lax.broadcasted_iota(jnp.int32, (1, width), 1) // HEAD_DIM
    for h in range(heads):
        skip_row = jnp.where(head_lane == h, skip_gain[h], skip_row)

    reach = TILE + HALO
    offset = lax.broadcasted_iota(jnp.int32, (TILE, reach), 1) - lax.broadcasted_iota(
        jnp.int32, (TILE, reach), 0
    )
    bands = [jnp.where(offset == HALO - j, 1.0, 0.0).astype(F32) for j in range(1, CONV)]
    taps = [xw_ref[...] * 0.5] + [
        bcw_ref[:, pl.ds(at, STATE)] * 0.5 for at in (b_at, c_at)
    ]
    conv_bias = [xb_ref[...] * 0.5] + [bcb_ref[:, pl.ds(at, STATE)] * 0.5 for at in (b_at, c_at)]
    part_at = [(0, width), (width, STATE), (width + STATE, STATE)]

    def conv_tile(i, parts):
        at = i * TILE
        ok = left_ext[:, at : at + reach]
        shift = jnp.concatenate(
            [jnp.where(ok >= j, bands[j - 1], 0.0) for j in range(1, CONV)], axis=0
        ).astype(BF16)
        for part in parts:
            begin_at, size = part_at[part]
            source = ext[at : at + reach, begin_at : begin_at + size]
            moved = dot(shift, source, ((1,), (0,)))
            h = conv_bias[part] + taps[part][3:4] * source[HALO:].astype(F32)
            h = h + taps[part][2:3] * moved[:TILE]
            h = h + taps[part][1:2] * moved[TILE : 2 * TILE]
            h = h + taps[part][0:1] * moved[2 * TILE :]
            mixed[at : at + TILE, begin_at : begin_at + size] = silu_half(h).astype(BF16)

    loads[0].wait()
    loads[1].wait()
    for i in range(1, tiles):
        conv_tile(i, (0, 1))

    @pl.when(ctx > 0)
    def _():
        for i in range(3):
            halo_copy(i).wait_recv()

    conv_tile(0, (0, 1))

    state = jnp.zeros((STATE, width), F32)
    for c in range(blocks):
        at = c * BLOCK
        state_buf[c] = state
        x_tail = (mixed[at : at + BLOCK, :width].astype(F32) * tail_buf[at : at + BLOCK, :]).astype(
            BF16
        )
        summary = dot(mixed[at : at + BLOCK, width : width + STATE], x_tail, ((0,), (0,)))
        state = state * decay_rows[c] + summary
    end_buf[...] = state
    shard_decay = decay_rows[0]
    for c in range(1, blocks):
        shard_decay = shard_decay * decay_rows[c]

    chunk = STATE // CHUNKS

    def state_copy(i):
        at = pl.ds(i * chunk, chunk)
        return pltpu.make_async_remote_copy(
            src_ref=send_buf.at[at, :],
            dst_ref=recv_buf.at[at, :],
            send_sem=state_send.at[i],
            recv_sem=state_recv.at[i],
            device_id=right,
            device_id_type=pl.DeviceIdType.MESH,
        )

    @pl.when(ctx == 0)
    def _():
        for i in range(CHUNKS):
            at = pl.ds(i * chunk, chunk)
            send_buf[at, :] = end_buf[at, :].astype(BF16)
            state_copy(i).start()

    def forward(stage):
        mine = ctx == stage if stage < blocks else ctx >= stage

        @pl.when(mine & not_last)
        def _():
            for i in range(CHUNKS):
                at = pl.ds(i * chunk, chunk)
                state_copy(i).wait_recv()
                send_buf[at, :] = (
                    end_buf[at, :] + shard_decay * recv_buf[at, :].astype(F32)
                ).astype(BF16)
                state_copy(i).start()

    loads[2].wait()
    loads[3].wait()
    gap_at = lax.broadcasted_iota(jnp.int32, (BLOCK, BLOCK), 0) - lax.broadcasted_iota(
        jnp.int32, (BLOCK, BLOCK), 1
    )
    for c in range(blocks):
        at = c * BLOCK
        for i in range(BLOCK // TILE):
            conv_tile(c * (BLOCK // TILE) + i, (2,))
        x_c = mixed[at : at + BLOCK, :width]
        b_c = mixed[at : at + BLOCK, width : width + STATE]
        c_c = mixed[at : at + BLOCK, width + STATE :]
        inner = dot(c_c, b_c, ((1,), (1,)))
        inner = jnp.where((gap_at >= 0) & (gap_at <= left[:, at : at + BLOCK]), inner, 0.0)
        y = skip_row * x_c.astype(F32)
        for h in range(heads):
            r = c * heads + h
            gap = jnp.minimum(run_col[:, r : r + 1] - run[r : r + 1], 0.0)
            mix = jnp.exp2(gap) * inner * step[h : h + 1, at : at + BLOCK]
            x_h = x_c * (head_lane == h).astype(F32).astype(BF16)
            y = y + dot(mix.astype(BF16), x_h, ((1,), (0,)))
        y_buf[at : at + BLOCK, :] = y
        gate_buf[at : at + BLOCK, :] = silu_half(z_buf[at : at + BLOCK, :].astype(F32) * 0.5)
        forward(c + 1)

    @pl.when(ctx == n_ctx - 1)
    def _():
        for i in range(CHUNKS):
            state_copy(i).wait_recv()

    entering = recv_buf[...].astype(F32)
    so_far = jnp.ones((1, width), F32)
    ones = jnp.ones((8, width), BF16)
    slot_row = lax.broadcasted_iota(jnp.int32, (tiles, TILE), 0)
    squares = jnp.zeros((tiles, TILE), F32)
    for c in range(blocks):
        at = c * BLOCK
        incoming = (state_buf[c] + so_far * entering).astype(BF16)
        so_far = so_far * decay_rows[c]
        from_state = dot(mixed[at : at + BLOCK, width + STATE :], incoming, ((1,), (0,)))
        y = y_buf[at : at + BLOCK, :] + entry_buf[at : at + BLOCK, :] * from_state
        gated = y * gate_buf[at : at + BLOCK, :]
        y_buf[at : at + BLOCK, :] = gated
        row = dot(ones, (gated * gated).astype(BF16), ((1,), (1,)))
        for i in range(BLOCK // TILE):
            squares = jnp.where(
                slot_row == c * (BLOCK // TILE) + i, row[0:1, i * TILE : (i + 1) * TILE], squares
            )
    sums[me] = squares

    def sums_copy(d):
        return pltpu.make_async_remote_copy(
            src_ref=sums.at[me],
            dst_ref=sums.at[me],
            send_sem=sums_send.at[d],
            recv_sem=sums_recv.at[d],
            device_id=(ctx, peers[d]),
            device_id_type=pl.DeviceIdType.MESH,
        )

    for d in range(n_head - 1):
        sums_copy(d).start()
    for d in range(n_head - 1):
        sums_copy(d).wait_recv()
    every = sums[0]
    for d in range(1, n_head):
        every = every + sums[d]
    scale = lax.rsqrt(every / (n_head * width) + NORM_FLOOR)
    norm_row = nw_ref[...]
    stores = []
    for c in range(blocks):
        at = c * BLOCK
        for i in range(BLOCK // TILE):
            t = c * (BLOCK // TILE) + i
            column = jnp.transpose(jnp.broadcast_to(scale[t : t + 1, :], (TILE, TILE)))
            column = jnp.concatenate([column] * (width // TILE), axis=1)
            piece = y_buf[t * TILE : (t + 1) * TILE, :] * column * norm_row
            out_buf[t * TILE : (t + 1) * TILE, :] = piece.astype(BF16)
        store = pltpu.make_async_copy(
            out_buf.at[pl.ds(at, BLOCK), :], out_hbm.at[pl.ds(at, BLOCK), :], out_sems.at[c]
        )
        store.start()
        stores.append(store)

    for d in range(n_head - 1):
        sums_copy(d).wait_send()

    @pl.when(not_last)
    def _():
        for i in range(3):
            halo_copy(i).wait_send()
        for i in range(CHUNKS):
            state_copy(i).wait_send()

    for store in stores:
        store.wait()


def shards(
    x_in,
    bc_in,
    z_in,
    dt_in,
    conv_x_w,
    conv_x_b,
    conv_bc_w,
    conv_bc_b,
    dt_bias,
    a_log,
    skip_gain,
    norm_w,
    doc_len,
):
    rows, width = x_in.shape
    n_ctx = lax.axis_size("context")
    n_head = lax.axis_size("head")
    blocks = rows // BLOCK
    tiles = rows // TILE
    anywhere = pl.BlockSpec(memory_space=pltpu.HBM)
    vmem = pl.BlockSpec(memory_space=pltpu.VMEM)
    smem = pl.BlockSpec(memory_space=pltpu.SMEM)
    dma = pltpu.SemaphoreType.DMA
    return pl.pallas_call(
        functools.partial(layer_kernel, n_ctx, n_head),
        out_shape=jax.ShapeDtypeStruct((rows, width), BF16),
        in_specs=[anywhere] * 3 + [vmem] * 5 + [smem] * 3 + [vmem, smem],
        out_specs=anywhere,
        scratch_shapes=[
            pltpu.VMEM((rows + HALO, width + 2 * STATE), BF16),
            pltpu.VMEM((rows, width), BF16),
            pltpu.VMEM((rows, width + 2 * STATE), BF16),
            pltpu.VMEM((rows, width), F32),
            pltpu.VMEM((rows, width), F32),
            pltpu.VMEM((blocks, STATE, width), F32),
            pltpu.VMEM((STATE, width), F32),
            pltpu.VMEM((rows, width), F32),
            pltpu.VMEM((rows, width), F32),
            pltpu.VMEM((STATE, width), BF16),
            pltpu.VMEM((STATE, width), BF16),
            pltpu.VMEM((n_head, tiles, TILE), F32),
            pltpu.VMEM((rows, width), BF16),
            dma((4,)),
            dma((3,)),
            dma((3,)),
            dma((CHUNKS,)),
            dma((CHUNKS,)),
            dma((n_head - 1,)),
            dma((n_head - 1,)),
            dma((blocks,)),
        ],
        compiler_params=pltpu.CompilerParams(
            collective_id=0, has_side_effects=True, vmem_limit_bytes=40 * 1024 * 1024
        ),
    )(
        x_in,
        bc_in,
        z_in,
        dt_in,
        conv_x_w,
        conv_x_b.reshape(1, -1),
        conv_bc_w,
        conv_bc_b.reshape(1, -1),
        dt_bias,
        a_log,
        skip_gain,
        norm_w.reshape(1, -1),
        doc_len,
    )


def solution(mesh):
    return jax.shard_map(
        shards,
        mesh=mesh,
        in_specs=(
            P("context", "head"),
            P("context", None),
            P("context", "head"),
            P("head", "context"),
            P(None, "head"),
            P("head"),
            P(),
            P(),
            P("head"),
            P("head"),
            P("head"),
            P("head"),
            P(),
        ),
        out_specs=P("context", "head"),
        check_vma=False,
    )
```

```python
import functools
import math

import jax
import jax.numpy as jnp
from jax import lax
from jax.experimental import pallas as pl
from jax.experimental.pallas import tpu as pltpu
from jax.sharding import PartitionSpec as P

HEAD_DIM = 64
STATE = 256
GROUPS = 8
CONV = 4
BLOCK = 256
TILE = 128
HALO = 16
CHUNKS = 8
LOG2E = math.log2(math.e)
NORM_FLOOR = 1e-05
F32 = jnp.float32
BF16 = jnp.bfloat16


def dot(a, b, dims):
    return lax.dot_general(a, b, (dims, ((), ())), preferred_element_type=F32)


def silu_half(h):
    return h + h * jnp.tanh(h)


def split_rows(v, parts):
    pieces = []
    for _ in range(parts):
        piece = v.astype(BF16).astype(F32)
        pieces.append(piece)
        v = v - piece
    return jnp.concatenate(pieces, axis=0).astype(BF16)


def layer_kernel(
    n_ctx,
    n_head,
    x_hbm,
    bc_hbm,
    z_hbm,
    dt_hbm,
    xw_hbm,
    xb_hbm,
    bcw_hbm,
    bcb_hbm,
    dt_bias_hbm,
    a_log_hbm,
    skip_hbm,
    nw_hbm,
    doc_hbm,
    out_hbm,
    dt_ref,
    taps_buf,
    bias_buf,
    nw_ref,
    dt_bias,
    a_log,
    skip_gain,
    doc_len,
    shift_buf,
    ext,
    z_buf,
    mixed,
    tail_buf,
    entry_buf,
    state_buf,
    end_buf,
    y_buf,
    gate_buf,
    send_buf,
    recv_buf,
    sums,
    out_buf,
    load_sems,
    small_sems,
    halo_send,
    halo_recv,
    state_send,
    state_recv,
    sums_send,
    sums_recv,
    out_sems,
):
    rows = x_hbm.shape[0]
    width = x_hbm.shape[1]
    heads = dt_ref.shape[0]
    docs = doc_len.shape[0]
    blocks = rows // BLOCK
    tiles = rows // TILE
    ctx = lax.axis_index("context")
    me = lax.axis_index("head")
    per_group = n_head * heads // GROUPS
    group = me * heads // per_group
    b_at = pl.multiple_of(group * STATE, STATE)
    c_at = pl.multiple_of((GROUPS + group) * STATE, STATE)
    not_last = ctx < n_ctx - 1

    barrier = pltpu.get_barrier_semaphore()

    @pl.when(ctx > 0)
    def _():
        pl.semaphore_signal(
            barrier, inc=1, device_id=(ctx - 1, me), device_id_type=pl.DeviceIdType.MESH
        )

    peers = [lax.rem(me + d, n_head) for d in range(1, n_head)]
    for peer in peers:
        pl.semaphore_signal(
            barrier, inc=1, device_id=(ctx, peer), device_id_type=pl.DeviceIdType.MESH
        )

    pairs = [
        (doc_hbm, doc_len),
        (dt_hbm, dt_ref),
        (dt_bias_hbm, dt_bias),
        (a_log_hbm, a_log),
        (skip_hbm, skip_gain),
        (xw_hbm, taps_buf.at[0]),
        (bcw_hbm.at[:, pl.ds(b_at, STATE)], taps_buf.at[1]),
        (bcw_hbm.at[:, pl.ds(c_at, STATE)], taps_buf.at[2]),
        (xb_hbm, bias_buf.at[0]),
        (bcb_hbm.at[:, pl.ds(b_at, STATE)], bias_buf.at[1]),
        (bcb_hbm.at[:, pl.ds(c_at, STATE)], bias_buf.at[2]),
        (nw_hbm, nw_ref),
    ]
    smalls = [
        pltpu.make_async_copy(src, dst, small_sems.at[i]) for i, (src, dst) in enumerate(pairs)
    ]
    for small in smalls:
        small.start()

    own = pl.ds(HALO, rows)
    loads = [
        pltpu.make_async_copy(x_hbm, ext.at[own, pl.ds(0, width)], load_sems.at[0]),
        pltpu.make_async_copy(
            bc_hbm.at[:, pl.ds(b_at, STATE)], ext.at[own, pl.ds(width, STATE)], load_sems.at[1]
        ),
        pltpu.make_async_copy(
            bc_hbm.at[:, pl.ds(c_at, STATE)],
            ext.at[own, pl.ds(width + STATE, STATE)],
            load_sems.at[2],
        ),
        pltpu.make_async_copy(z_hbm, z_buf, load_sems.at[3]),
    ]
    for load in loads:
        load.start()

    @pl.when(ctx == 0)
    def _():
        ext[pl.ds(0, HALO), :] = jnp.zeros((HALO, width + 2 * STATE), BF16)
        recv_buf[...] = jnp.zeros((STATE, width), BF16)

    for small in smalls:
        small.wait()

    first = ctx * rows
    ends, begins, total = [], [], jnp.int32(0)
    for d in range(docs):
        begins.append(total)
        total = total + doc_len[d]
        ends.append(total)

    def tokens_left(pos):
        end = jnp.zeros_like(pos)
        for d in reversed(range(docs)):
            end = jnp.where(pos < ends[d], ends[d], end)
        return jnp.where(pos < 0, -1, end - 1 - pos)

    ext_lanes = rows + TILE
    left_ext = tokens_left(first - HALO + lax.broadcasted_iota(jnp.int32, (1, ext_lanes), 1))
    lane = lax.broadcasted_iota(jnp.int32, (1, rows), 1)
    pos = first + lane
    left = tokens_left(pos)
    begin = jnp.zeros_like(pos)
    for d in range(docs):
        begin = jnp.where(pos >= begins[d], begins[d], begin)
    lane_b = lax.rem(lane, BLOCK)
    alive = pos - begin > lane_b
    tail_same = left >= BLOCK - 1 - lane_b

    head_row = lax.broadcasted_iota(jnp.int32, (heads, rows), 0)
    bias_col = jnp.zeros((heads, rows), F32)
    alog_col = jnp.zeros((heads, rows), F32)
    for h in range(heads):
        bias_col = jnp.where(head_row == h, dt_bias[h], bias_col)
        alog_col = jnp.where(head_row == h, a_log[h], alog_col)
    raw = dt_ref[...].astype(F32) + bias_col
    step = jnp.maximum(raw, 0.0) + jnp.log1p(jnp.exp(-jnp.abs(raw)))
    log_decay = step * (jnp.exp(alog_col) * (-LOG2E))
    per_block = jnp.concatenate(
        [log_decay[:, c * BLOCK : (c + 1) * BLOCK] for c in range(blocks)], axis=0
    )
    upper = (
        lax.broadcasted_iota(jnp.int32, (BLOCK, BLOCK), 0)
        <= lax.broadcasted_iota(jnp.int32, (BLOCK, BLOCK), 1)
    )
    n_run = blocks * heads
    summed = dot(split_rows(per_block, 3), upper.astype(F32).astype(BF16), ((1,), (0,)))
    run = summed[:n_run] + summed[n_run : 2 * n_run] + summed[2 * n_run :]
    run_col = jnp.transpose(run)
    ends_run = run[:, BLOCK - 1 : BLOCK]
    running = jnp.concatenate([run[c * heads : (c + 1) * heads] for c in range(blocks)], axis=1)
    to_end = jnp.concatenate(
        [
            ends_run[c * heads : (c + 1) * heads] - run[c * heads : (c + 1) * heads]
            for c in range(blocks)
        ],
        axis=1,
    )
    tail_rows = jnp.where(tail_same, jnp.exp2(to_end), 0.0) * step
    entry_rows = jnp.where(alive, jnp.exp2(running), 0.0)

    spread = (
        lax.broadcasted_iota(jnp.int32, (heads, width), 0)
        == lax.broadcasted_iota(jnp.int32, (heads, width), 1) // HEAD_DIM
    ).astype(F32)
    spread2 = jnp.concatenate([spread, spread], axis=0).astype(BF16)
    tail_buf[...] = dot(split_rows(tail_rows, 2), spread2, ((0,), (0,)))

    decay_rows = []
    for c in range(blocks):
        at = c * BLOCK + BLOCK - 1
        decay_rows.append(jnp.sum(entry_rows[:, at : at + 1] * spread, axis=0, keepdims=True))
    skip_row = jnp.zeros((1, width), F32)
    head_lane = lax.broadcasted_iota(jnp.int32, (1, width), 1) // HEAD_DIM
    for h in range(heads):
        skip_row = jnp.where(head_lane == h, skip_gain[h], skip_row)

    pl.semaphore_wait(barrier, n_head - 1 + jnp.where(not_last, 1, 0))

    right = (jnp.minimum(ctx + 1, n_ctx - 1), me)
    last_rows = pl.ds(rows - HALO, HALO)
    halo_src = [
        x_hbm.at[last_rows, :],
        bc_hbm.at[last_rows, pl.ds(b_at, STATE)],
        bc_hbm.at[last_rows, pl.ds(c_at, STATE)],
    ]
    halo_at = [pl.ds(0, width), pl.ds(width, STATE), pl.ds(width + STATE, STATE)]

    def halo_copy(i):
        return pltpu.make_async_remote_copy(
            src_ref=halo_src[i],
            dst_ref=ext.at[pl.ds(0, HALO), halo_at[i]],
            send_sem=halo_send.at[i],
            recv_sem=halo_recv.at[i],
            device_id=right,
            device_id_type=pl.DeviceIdType.MESH,
        )

    @pl.when(not_last)
    def _():
        for i in range(3):
            halo_copy(i).start()

    reach = TILE + HALO
    offset = lax.broadcasted_iota(jnp.int32, (TILE, reach), 1) - lax.broadcasted_iota(
        jnp.int32, (TILE, reach), 0
    )
    bands = [jnp.where(offset == HALO - j, 1.0, 0.0).astype(F32) for j in range(1, CONV)]
    taps = [taps_buf[i] * 0.5 for i in range(3)]
    conv_bias = [bias_buf[i] * 0.5 for i in range(3)]
    part_at = [(0, width), (width, STATE), (width + STATE, STATE)]

    def conv_tile(i, parts):
        at = i * TILE
        if 0 in parts:
            ok = left_ext[:, at : at + reach]
            shift = jnp.concatenate(
                [jnp.where(ok >= j, bands[j - 1], 0.0) for j in range(1, CONV)], axis=0
            ).astype(BF16)
            shift_buf[i] = shift
        else:
            shift = shift_buf[i]
        for part in parts:
            begin_at, size = part_at[part]
            source = ext[at : at + reach, begin_at : begin_at + size]
            moved = dot(shift, source, ((1,), (0,)))
            h = conv_bias[part] + taps[part][3:4] * source[HALO:].astype(F32)
            h = h + taps[part][2:3] * moved[:TILE]
            h = h + taps[part][1:2] * moved[TILE : 2 * TILE]
            h = h + taps[part][0:1] * moved[2 * TILE :]
            mixed[at : at + TILE, begin_at : begin_at + size] = silu_half(h).astype(BF16)

    loads[0].wait()
    loads[1].wait()
    for i in range(1, tiles):
        conv_tile(i, (0, 1))

    @pl.when(ctx > 0)
    def _():
        for i in range(3):
            halo_copy(i).wait_recv()

    conv_tile(0, (0, 1))

    state = jnp.zeros((STATE, width), F32)
    for c in range(blocks):
        at = c * BLOCK
        state_buf[c] = state
        x_tail = (mixed[at : at + BLOCK, :width].astype(F32) * tail_buf[at : at + BLOCK, :]).astype(
            BF16
        )
        summary = dot(mixed[at : at + BLOCK, width : width + STATE], x_tail, ((0,), (0,)))
        state = state * decay_rows[c] + summary
    end_buf[...] = state
    shard_decay = decay_rows[0]
    for c in range(1, blocks):
        shard_decay = shard_decay * decay_rows[c]

    chunk = STATE // CHUNKS

    def state_copy(i):
        at = pl.ds(i * chunk, chunk)
        return pltpu.make_async_remote_copy(
            src_ref=send_buf.at[at, :],
            dst_ref=recv_buf.at[at, :],
            send_sem=state_send.at[i],
            recv_sem=state_recv.at[i],
            device_id=right,
            device_id_type=pl.DeviceIdType.MESH,
        )

    @pl.when(ctx == 0)
    def _():
        for i in range(CHUNKS):
            at = pl.ds(i * chunk, chunk)
            send_buf[at, :] = end_buf[at, :].astype(BF16)
            state_copy(i).start()

    def forward(stage):
        mine = ctx == stage if stage < blocks else ctx >= stage

        @pl.when(mine & not_last)
        def _():
            for i in range(CHUNKS):
                at = pl.ds(i * chunk, chunk)
                state_copy(i).wait_recv()
                send_buf[at, :] = (
                    end_buf[at, :] + shard_decay * recv_buf[at, :].astype(F32)
                ).astype(BF16)
                state_copy(i).start()

    entry_buf[...] = dot(split_rows(entry_rows, 2), spread2, ((0,), (0,)))
    loads[2].wait()
    loads[3].wait()
    gap_at = lax.broadcasted_iota(jnp.int32, (BLOCK, BLOCK), 0) - lax.broadcasted_iota(
        jnp.int32, (BLOCK, BLOCK), 1
    )
    for c in range(blocks):
        at = c * BLOCK
        for i in range(BLOCK // TILE):
            conv_tile(c * (BLOCK // TILE) + i, (2,))
        x_c = mixed[at : at + BLOCK, :width]
        b_c = mixed[at : at + BLOCK, width : width + STATE]
        c_c = mixed[at : at + BLOCK, width + STATE :]
        inner = dot(c_c, b_c, ((1,), (1,)))
        inner = jnp.where((gap_at >= 0) & (gap_at <= left[:, at : at + BLOCK]), inner, 0.0)
        x_heads = [x_c * (head_lane == h).astype(F32).astype(BF16) for h in range(heads)]
        for lo in range(0, BLOCK, TILE):
            hi = lo + TILE
            y = skip_row * x_c[lo:hi].astype(F32)
            for h in range(heads):
                r = c * heads + h
                gap = jnp.minimum(run_col[lo:hi, r : r + 1] - run[r : r + 1, :hi], 0.0)
                mix = jnp.exp2(gap) * inner[lo:hi, :hi] * step[h : h + 1, at : at + hi]
                y = y + dot(mix.astype(BF16), x_heads[h][:hi], ((1,), (0,)))
            y_buf[at + lo : at + hi, :] = y
        gate_buf[at : at + BLOCK, :] = silu_half(z_buf[at : at + BLOCK, :].astype(F32) * 0.5)
        forward(c + 1)

    @pl.when(ctx == n_ctx - 1)
    def _():
        for i in range(CHUNKS):
            state_copy(i).wait_recv()

    entering = recv_buf[...].astype(F32)
    so_far = jnp.ones((1, width), F32)
    ones = jnp.ones((8, width), BF16)
    slot_row = lax.broadcasted_iota(jnp.int32, (tiles, TILE), 0)
    squares = jnp.zeros((tiles, TILE), F32)
    for c in range(blocks):
        at = c * BLOCK
        incoming = (state_buf[c] + so_far * entering).astype(BF16)
        so_far = so_far * decay_rows[c]
        from_state = dot(mixed[at : at + BLOCK, width + STATE :], incoming, ((1,), (0,)))
        y = y_buf[at : at + BLOCK, :] + entry_buf[at : at + BLOCK, :] * from_state
        gated = y * gate_buf[at : at + BLOCK, :]
        y_buf[at : at + BLOCK, :] = gated
        row = dot(ones, (gated * gated).astype(BF16), ((1,), (1,)))
        for i in range(BLOCK // TILE):
            squares = jnp.where(
                slot_row == c * (BLOCK // TILE) + i, row[0:1, i * TILE : (i + 1) * TILE], squares
            )
    sums[me] = squares

    def sums_copy(d):
        return pltpu.make_async_remote_copy(
            src_ref=sums.at[me],
            dst_ref=sums.at[me],
            send_sem=sums_send.at[d],
            recv_sem=sums_recv.at[d],
            device_id=(ctx, peers[d]),
            device_id_type=pl.DeviceIdType.MESH,
        )

    for d in range(n_head - 1):
        sums_copy(d).start()
    for d in range(n_head - 1):
        sums_copy(d).wait_recv()
    every = sums[0]
    for d in range(1, n_head):
        every = every + sums[d]
    scale = lax.rsqrt(every / (n_head * width) + NORM_FLOOR)
    norm_row = nw_ref[...]
    stores = []
    for c in range(blocks):
        at = c * BLOCK
        for i in range(BLOCK // TILE):
            t = c * (BLOCK // TILE) + i
            column = jnp.transpose(jnp.broadcast_to(scale[t : t + 1, :], (TILE, TILE)))
            column = jnp.concatenate([column] * (width // TILE), axis=1)
            piece = y_buf[t * TILE : (t + 1) * TILE, :] * column * norm_row
            out_buf[t * TILE : (t + 1) * TILE, :] = piece.astype(BF16)
        store = pltpu.make_async_copy(
            out_buf.at[pl.ds(at, BLOCK), :], out_hbm.at[pl.ds(at, BLOCK), :], out_sems.at[c]
        )
        store.start()
        stores.append(store)

    for d in range(n_head - 1):
        sums_copy(d).wait_send()

    @pl.when(not_last)
    def _():
        for i in range(3):
            halo_copy(i).wait_send()
        for i in range(CHUNKS):
            state_copy(i).wait_send()

    for store in stores:
        store.wait()


def shards(
    x_in,
    bc_in,
    z_in,
    dt_in,
    conv_x_w,
    conv_x_b,
    conv_bc_w,
    conv_bc_b,
    dt_bias,
    a_log,
    skip_gain,
    norm_w,
    doc_len,
):
    rows, width = x_in.shape
    n_ctx = lax.axis_size("context")
    n_head = lax.axis_size("head")
    blocks = rows // BLOCK
    tiles = rows // TILE
    anywhere = pl.BlockSpec(memory_space=pltpu.HBM)
    heads = dt_in.shape[0]
    docs = doc_len.shape[0]
    dma = pltpu.SemaphoreType.DMA
    return pl.pallas_call(
        functools.partial(layer_kernel, n_ctx, n_head),
        out_shape=jax.ShapeDtypeStruct((rows, width), BF16),
        in_specs=[anywhere] * 13,
        out_specs=anywhere,
        scratch_shapes=[
            pltpu.VMEM((heads, rows), BF16),
            pltpu.VMEM((3, CONV, width), F32),
            pltpu.VMEM((3, 1, width), F32),
            pltpu.VMEM((1, width), F32),
            pltpu.SMEM((heads,), F32),
            pltpu.SMEM((heads,), F32),
            pltpu.SMEM((heads,), F32),
            pltpu.SMEM((docs,), jnp.int32),
            pltpu.VMEM((tiles, (CONV - 1) * TILE, TILE + HALO), BF16),
            pltpu.VMEM((rows + HALO, width + 2 * STATE), BF16),
            pltpu.VMEM((rows, width), BF16),
            pltpu.VMEM((rows, width + 2 * STATE), BF16),
            pltpu.VMEM((rows, width), F32),
            pltpu.VMEM((rows, width), F32),
            pltpu.VMEM((blocks, STATE, width), F32),
            pltpu.VMEM((STATE, width), F32),
            pltpu.VMEM((rows, width), F32),
            pltpu.VMEM((rows, width), F32),
            pltpu.VMEM((STATE, width), BF16),
            pltpu.VMEM((STATE, width), BF16),
            pltpu.VMEM((n_head, tiles, TILE), F32),
            pltpu.VMEM((rows, width), BF16),
            dma((4,)),
            dma((12,)),
            dma((3,)),
            dma((3,)),
            dma((CHUNKS,)),
            dma((CHUNKS,)),
            dma((n_head - 1,)),
            dma((n_head - 1,)),
            dma((blocks,)),
        ],
        compiler_params=pltpu.CompilerParams(
            collective_id=0, has_side_effects=True, vmem_limit_bytes=60 * 1024 * 1024
        ),
    )(
        x_in,
        bc_in,
        z_in,
        dt_in,
        conv_x_w,
        conv_x_b.reshape(1, -1),
        conv_bc_w,
        conv_bc_b.reshape(1, -1),
        dt_bias,
        a_log,
        skip_gain,
        norm_w.reshape(1, -1),
        doc_len,
    )


def solution(mesh):
    return jax.shard_map(
        shards,
        mesh=mesh,
        in_specs=(
            P("context", "head"),
            P("context", None),
            P("context", "head"),
            P("head", "context"),
            P(None, "head"),
            P("head"),
            P(),
            P(),
            P("head"),
            P("head"),
            P("head"),
            P("head"),
            P(),
        ),
        out_specs=P("context", "head"),
        check_vma=False,
    )
```

```python
import functools
import math

import jax
import jax.numpy as jnp
from jax import lax
from jax.experimental import pallas as pl
from jax.experimental.pallas import tpu as pltpu
from jax.sharding import PartitionSpec as P

HEAD_DIM = 64
STATE = 256
GROUPS = 8
CONV = 4
BLOCK = 256
TILE = 128
HALO = 16
CHUNKS = 8
LOG2E = math.log2(math.e)
NORM_FLOOR = 1e-05
F32 = jnp.float32
BF16 = jnp.bfloat16


def dot(a, b, dims):
    return lax.dot_general(a, b, (dims, ((), ())), preferred_element_type=F32)


def silu_half(h):
    return h + h * jnp.tanh(h)


def split_rows(v, parts):
    pieces = []
    for _ in range(parts):
        piece = v.astype(BF16).astype(F32)
        pieces.append(piece)
        v = v - piece
    return jnp.concatenate(pieces, axis=0).astype(BF16)


def layer_kernel(
    n_ctx,
    n_head,
    x_hbm,
    bc_hbm,
    z_hbm,
    dt_hbm,
    xw_hbm,
    xb_hbm,
    bcw_hbm,
    bcb_hbm,
    dt_bias_hbm,
    a_log_hbm,
    skip_hbm,
    nw_hbm,
    doc_hbm,
    gated_ref,
    scale_ref,
    dt_ref,
    taps_buf,
    bias_buf,
    nw_ref,
    dt_bias,
    a_log,
    skip_gain,
    doc_len,
    shift_buf,
    ext,
    z_buf,
    mixed,
    tail_buf,
    entry_buf,
    state_buf,
    end_buf,
    y_buf,
    gate_buf,
    send_buf,
    recv_buf,
    sums,
    load_sems,
    small_sems,
    halo_send,
    halo_recv,
    state_send,
    state_recv,
    sums_send,
    sums_recv,
):
    rows = x_hbm.shape[0]
    width = x_hbm.shape[1]
    heads = dt_ref.shape[0]
    docs = doc_len.shape[0]
    blocks = rows // BLOCK
    tiles = rows // TILE
    ctx = lax.axis_index("context")
    me = lax.axis_index("head")
    per_group = n_head * heads // GROUPS
    group = me * heads // per_group
    b_at = pl.multiple_of(group * STATE, STATE)
    c_at = pl.multiple_of((GROUPS + group) * STATE, STATE)
    not_last = ctx < n_ctx - 1

    barrier = pltpu.get_barrier_semaphore()

    @pl.when(ctx > 0)
    def _():
        pl.semaphore_signal(
            barrier, inc=1, device_id=(ctx - 1, me), device_id_type=pl.DeviceIdType.MESH
        )

    peers = [lax.rem(me + d, n_head) for d in range(1, n_head)]
    for peer in peers:
        pl.semaphore_signal(
            barrier, inc=1, device_id=(ctx, peer), device_id_type=pl.DeviceIdType.MESH
        )

    pairs = [
        (doc_hbm, doc_len),
        (dt_hbm, dt_ref),
        (dt_bias_hbm, dt_bias),
        (a_log_hbm, a_log),
        (skip_hbm, skip_gain),
        (xw_hbm, taps_buf.at[0]),
        (bcw_hbm.at[:, pl.ds(b_at, STATE)], taps_buf.at[1]),
        (bcw_hbm.at[:, pl.ds(c_at, STATE)], taps_buf.at[2]),
        (xb_hbm, bias_buf.at[0]),
        (bcb_hbm.at[:, pl.ds(b_at, STATE)], bias_buf.at[1]),
        (bcb_hbm.at[:, pl.ds(c_at, STATE)], bias_buf.at[2]),
        (nw_hbm, nw_ref),
    ]
    smalls = [
        pltpu.make_async_copy(src, dst, small_sems.at[i]) for i, (src, dst) in enumerate(pairs)
    ]
    for small in smalls:
        small.start()

    own = pl.ds(HALO, rows)
    loads = [
        pltpu.make_async_copy(x_hbm, ext.at[own, pl.ds(0, width)], load_sems.at[0]),
        pltpu.make_async_copy(
            bc_hbm.at[:, pl.ds(b_at, STATE)], ext.at[own, pl.ds(width, STATE)], load_sems.at[1]
        ),
        pltpu.make_async_copy(
            bc_hbm.at[:, pl.ds(c_at, STATE)],
            ext.at[own, pl.ds(width + STATE, STATE)],
            load_sems.at[2],
        ),
        pltpu.make_async_copy(z_hbm, z_buf, load_sems.at[3]),
    ]
    for load in loads:
        load.start()

    @pl.when(ctx == 0)
    def _():
        ext[pl.ds(0, HALO), :] = jnp.zeros((HALO, width + 2 * STATE), BF16)
        recv_buf[...] = jnp.zeros((STATE, width), BF16)

    for small in smalls:
        small.wait()

    first = ctx * rows
    ends, begins, total = [], [], jnp.int32(0)
    for d in range(docs):
        begins.append(total)
        total = total + doc_len[d]
        ends.append(total)

    def tokens_left(pos):
        end = jnp.zeros_like(pos)
        for d in reversed(range(docs)):
            end = jnp.where(pos < ends[d], ends[d], end)
        return jnp.where(pos < 0, -1, end - 1 - pos)

    ext_lanes = rows + TILE
    left_ext = tokens_left(first - HALO + lax.broadcasted_iota(jnp.int32, (1, ext_lanes), 1))
    lane = lax.broadcasted_iota(jnp.int32, (1, rows), 1)
    pos = first + lane
    left = tokens_left(pos)
    begin = jnp.zeros_like(pos)
    for d in range(docs):
        begin = jnp.where(pos >= begins[d], begins[d], begin)
    lane_b = lax.rem(lane, BLOCK)
    alive = pos - begin > lane_b
    tail_same = left >= BLOCK - 1 - lane_b

    head_row = lax.broadcasted_iota(jnp.int32, (heads, rows), 0)
    bias_col = jnp.zeros((heads, rows), F32)
    alog_col = jnp.zeros((heads, rows), F32)
    for h in range(heads):
        bias_col = jnp.where(head_row == h, dt_bias[h], bias_col)
        alog_col = jnp.where(head_row == h, a_log[h], alog_col)
    raw = dt_ref[...].astype(F32) + bias_col
    step = jnp.maximum(raw, 0.0) + jnp.log1p(jnp.exp(-jnp.abs(raw)))
    log_decay = step * (jnp.exp(alog_col) * (-LOG2E))
    per_block = jnp.concatenate(
        [log_decay[:, c * BLOCK : (c + 1) * BLOCK] for c in range(blocks)], axis=0
    )
    upper = (
        lax.broadcasted_iota(jnp.int32, (BLOCK, BLOCK), 0)
        <= lax.broadcasted_iota(jnp.int32, (BLOCK, BLOCK), 1)
    )
    n_run = blocks * heads
    summed = dot(split_rows(per_block, 3), upper.astype(F32).astype(BF16), ((1,), (0,)))
    run = summed[:n_run] + summed[n_run : 2 * n_run] + summed[2 * n_run :]
    run_col = jnp.transpose(run)
    ends_run = run[:, BLOCK - 1 : BLOCK]
    running = jnp.concatenate([run[c * heads : (c + 1) * heads] for c in range(blocks)], axis=1)
    to_end = jnp.concatenate(
        [
            ends_run[c * heads : (c + 1) * heads] - run[c * heads : (c + 1) * heads]
            for c in range(blocks)
        ],
        axis=1,
    )
    tail_rows = jnp.where(tail_same, jnp.exp2(to_end), 0.0) * step
    entry_rows = jnp.where(alive, jnp.exp2(running), 0.0)

    spread = (
        lax.broadcasted_iota(jnp.int32, (heads, width), 0)
        == lax.broadcasted_iota(jnp.int32, (heads, width), 1) // HEAD_DIM
    ).astype(F32)
    spread2 = jnp.concatenate([spread, spread], axis=0).astype(BF16)
    tail_buf[...] = dot(split_rows(tail_rows, 2), spread2, ((0,), (0,)))

    decay_rows = []
    for c in range(blocks):
        at = c * BLOCK + BLOCK - 1
        decay_rows.append(jnp.sum(entry_rows[:, at : at + 1] * spread, axis=0, keepdims=True))
    skip_row = jnp.zeros((1, width), F32)
    head_lane = lax.broadcasted_iota(jnp.int32, (1, width), 1) // HEAD_DIM
    for h in range(heads):
        skip_row = jnp.where(head_lane == h, skip_gain[h], skip_row)

    pl.semaphore_wait(barrier, n_head - 1 + jnp.where(not_last, 1, 0))

    right = (jnp.minimum(ctx + 1, n_ctx - 1), me)
    last_rows = pl.ds(rows - HALO, HALO)
    halo_src = [
        x_hbm.at[last_rows, :],
        bc_hbm.at[last_rows, pl.ds(b_at, STATE)],
        bc_hbm.at[last_rows, pl.ds(c_at, STATE)],
    ]
    halo_at = [pl.ds(0, width), pl.ds(width, STATE), pl.ds(width + STATE, STATE)]

    def halo_copy(i):
        return pltpu.make_async_remote_copy(
            src_ref=halo_src[i],
            dst_ref=ext.at[pl.ds(0, HALO), halo_at[i]],
            send_sem=halo_send.at[i],
            recv_sem=halo_recv.at[i],
            device_id=right,
            device_id_type=pl.DeviceIdType.MESH,
        )

    @pl.when(not_last)
    def _():
        for i in range(3):
            halo_copy(i).start()

    reach = TILE + HALO
    offset = lax.broadcasted_iota(jnp.int32, (TILE, reach), 1) - lax.broadcasted_iota(
        jnp.int32, (TILE, reach), 0
    )
    bands = [jnp.where(offset == HALO - j, 1.0, 0.0).astype(F32) for j in range(1, CONV)]
    taps = [taps_buf[i] * 0.5 for i in range(3)]
    conv_bias = [bias_buf[i] * 0.5 for i in range(3)]
    part_at = [(0, width), (width, STATE), (width + STATE, STATE)]

    def conv_tile(i, parts):
        at = i * TILE
        if 0 in parts:
            ok = left_ext[:, at : at + reach]
            shift = jnp.concatenate(
                [jnp.where(ok >= j, bands[j - 1], 0.0) for j in range(1, CONV)], axis=0
            ).astype(BF16)
            shift_buf[i] = shift
        else:
            shift = shift_buf[i]
        for part in parts:
            begin_at, size = part_at[part]
            source = ext[at : at + reach, begin_at : begin_at + size]
            moved = dot(shift, source, ((1,), (0,)))
            h = conv_bias[part] + taps[part][3:4] * source[HALO:].astype(F32)
            h = h + taps[part][2:3] * moved[:TILE]
            h = h + taps[part][1:2] * moved[TILE : 2 * TILE]
            h = h + taps[part][0:1] * moved[2 * TILE :]
            mixed[at : at + TILE, begin_at : begin_at + size] = silu_half(h).astype(BF16)

    loads[0].wait()
    loads[1].wait()
    for i in range(1, tiles):
        conv_tile(i, (0, 1))

    @pl.when(ctx > 0)
    def _():
        for i in range(3):
            halo_copy(i).wait_recv()

    conv_tile(0, (0, 1))

    state = jnp.zeros((STATE, width), F32)
    for c in range(blocks):
        at = c * BLOCK
        state_buf[c] = state
        x_tail = (mixed[at : at + BLOCK, :width].astype(F32) * tail_buf[at : at + BLOCK, :]).astype(
            BF16
        )
        summary = dot(mixed[at : at + BLOCK, width : width + STATE], x_tail, ((0,), (0,)))
        state = state * decay_rows[c] + summary
    end_buf[...] = state
    shard_decay = decay_rows[0]
    for c in range(1, blocks):
        shard_decay = shard_decay * decay_rows[c]

    chunk = STATE // CHUNKS

    def state_copy(i):
        at = pl.ds(i * chunk, chunk)
        return pltpu.make_async_remote_copy(
            src_ref=send_buf.at[at, :],
            dst_ref=recv_buf.at[at, :],
            send_sem=state_send.at[i],
            recv_sem=state_recv.at[i],
            device_id=right,
            device_id_type=pl.DeviceIdType.MESH,
        )

    @pl.when(ctx == 0)
    def _():
        for i in range(CHUNKS):
            at = pl.ds(i * chunk, chunk)
            send_buf[at, :] = end_buf[at, :].astype(BF16)
            state_copy(i).start()

    half = CHUNKS // 2

    def forward(stage):
        early = stage <= 2
        mine = (ctx == 1) if early else (ctx >= 2)
        begin_at = half * ((stage - 1) % 2)

        @pl.when(mine & not_last)
        def _():
            for i in range(begin_at, begin_at + half):
                at = pl.ds(i * chunk, chunk)
                state_copy(i).wait_recv()
                send_buf[at, :] = (
                    end_buf[at, :] + shard_decay * recv_buf[at, :].astype(F32)
                ).astype(BF16)
                state_copy(i).start()

    entry_buf[...] = dot(split_rows(entry_rows, 2), spread2, ((0,), (0,)))
    loads[2].wait()
    loads[3].wait()
    gap_at = lax.broadcasted_iota(jnp.int32, (BLOCK, BLOCK), 0) - lax.broadcasted_iota(
        jnp.int32, (BLOCK, BLOCK), 1
    )
    for c in range(blocks):
        at = c * BLOCK
        for i in range(BLOCK // TILE):
            conv_tile(c * (BLOCK // TILE) + i, (2,))
        x_c = mixed[at : at + BLOCK, :width]
        b_c = mixed[at : at + BLOCK, width : width + STATE]
        c_c = mixed[at : at + BLOCK, width + STATE :]
        inner = dot(c_c, b_c, ((1,), (1,)))
        inner = jnp.where((gap_at >= 0) & (gap_at <= left[:, at : at + BLOCK]), inner, 0.0)
        x_heads = [x_c * (head_lane == h).astype(F32).astype(BF16) for h in range(heads)]
        for lo in range(0, BLOCK, TILE):
            hi = lo + TILE
            y = skip_row * x_c[lo:hi].astype(F32)
            for h in range(heads):
                r = c * heads + h
                gap = jnp.minimum(run_col[lo:hi, r : r + 1] - run[r : r + 1, :hi], 0.0)
                mix = jnp.exp2(gap) * inner[lo:hi, :hi] * step[h : h + 1, at : at + hi]
                y = y + dot(mix.astype(BF16), x_heads[h][:hi], ((1,), (0,)))
            y_buf[at + lo : at + hi, :] = y
        gate_buf[at : at + BLOCK, :] = silu_half(z_buf[at : at + BLOCK, :].astype(F32) * 0.5)
        forward(c + 1)

    @pl.when(ctx == n_ctx - 1)
    def _():
        for i in range(CHUNKS):
            state_copy(i).wait_recv()

    norm_row = nw_ref[...]
    entering = recv_buf[...].astype(F32)
    so_far = jnp.ones((1, width), F32)
    ones = jnp.ones((8, width), BF16)
    slot_row = lax.broadcasted_iota(jnp.int32, (tiles, TILE), 0)
    squares = jnp.zeros((tiles, TILE), F32)
    for c in range(blocks):
        at = c * BLOCK
        incoming = (state_buf[c] + so_far * entering).astype(BF16)
        so_far = so_far * decay_rows[c]
        from_state = dot(mixed[at : at + BLOCK, width + STATE :], incoming, ((1,), (0,)))
        y = y_buf[at : at + BLOCK, :] + entry_buf[at : at + BLOCK, :] * from_state
        gated = y * gate_buf[at : at + BLOCK, :]
        gated_ref[at : at + BLOCK, :] = gated * norm_row
        row = dot(ones, (gated * gated).astype(BF16), ((1,), (1,)))
        for i in range(BLOCK // TILE):
            squares = jnp.where(
                slot_row == c * (BLOCK // TILE) + i, row[0:1, i * TILE : (i + 1) * TILE], squares
            )
    sums[me] = squares

    def sums_copy(d):
        return pltpu.make_async_remote_copy(
            src_ref=sums.at[me],
            dst_ref=sums.at[me],
            send_sem=sums_send.at[d],
            recv_sem=sums_recv.at[d],
            device_id=(ctx, peers[d]),
            device_id_type=pl.DeviceIdType.MESH,
        )

    for d in range(n_head - 1):
        sums_copy(d).start()
    for d in range(n_head - 1):
        sums_copy(d).wait_recv()
    every = sums[0]
    for d in range(1, n_head):
        every = every + sums[d]
    scale_ref[...] = lax.rsqrt(every / (n_head * width) + NORM_FLOOR)

    for d in range(n_head - 1):
        sums_copy(d).wait_send()

    @pl.when(not_last)
    def _():
        for i in range(3):
            halo_copy(i).wait_send()
        for i in range(CHUNKS):
            state_copy(i).wait_send()


def scale_kernel(gated_ref, scale_ref, out_hbm, out_buf, out_sems):
    rows, width = gated_ref.shape
    stores = []
    for t in range(rows // TILE):
        at = pl.ds(t * TILE, TILE)
        column = jnp.transpose(jnp.broadcast_to(scale_ref[t : t + 1, :], (TILE, TILE)))
        column = jnp.concatenate([column] * (width // TILE), axis=1)
        out_buf[at, :] = (gated_ref[at, :] * column).astype(BF16)
        if t % 2 == 1:
            pair = pl.ds((t - 1) * TILE, 2 * TILE)
            store = pltpu.make_async_copy(
                out_buf.at[pair, :], out_hbm.at[pair, :], out_sems.at[t // 2]
            )
            store.start()
            stores.append(store)
    for store in stores:
        store.wait()


def shards(
    x_in,
    bc_in,
    z_in,
    dt_in,
    conv_x_w,
    conv_x_b,
    conv_bc_w,
    conv_bc_b,
    dt_bias,
    a_log,
    skip_gain,
    norm_w,
    doc_len,
):
    rows, width = x_in.shape
    n_ctx = lax.axis_size("context")
    n_head = lax.axis_size("head")
    blocks = rows // BLOCK
    tiles = rows // TILE
    anywhere = pl.BlockSpec(memory_space=pltpu.HBM)
    heads = dt_in.shape[0]
    docs = doc_len.shape[0]
    vmem = pl.BlockSpec(memory_space=pltpu.VMEM)
    dma = pltpu.SemaphoreType.DMA
    gated, scale = pl.pallas_call(
        functools.partial(layer_kernel, n_ctx, n_head),
        out_shape=(pltpu.VMEM((rows, width), F32), pltpu.VMEM((tiles, TILE), F32)),
        in_specs=[anywhere] * 13,
        out_specs=(vmem, vmem),
        scratch_shapes=[
            pltpu.VMEM((heads, rows), BF16),
            pltpu.VMEM((3, CONV, width), F32),
            pltpu.VMEM((3, 1, width), F32),
            pltpu.VMEM((1, width), F32),
            pltpu.SMEM((heads,), F32),
            pltpu.SMEM((heads,), F32),
            pltpu.SMEM((heads,), F32),
            pltpu.SMEM((docs,), jnp.int32),
            pltpu.VMEM((tiles, (CONV - 1) * TILE, TILE + HALO), BF16),
            pltpu.VMEM((rows + HALO, width + 2 * STATE), BF16),
            pltpu.VMEM((rows, width), BF16),
            pltpu.VMEM((rows, width + 2 * STATE), BF16),
            pltpu.VMEM((rows, width), F32),
            pltpu.VMEM((rows, width), F32),
            pltpu.VMEM((blocks, STATE, width), F32),
            pltpu.VMEM((STATE, width), F32),
            pltpu.VMEM((rows, width), F32),
            pltpu.VMEM((rows, width), F32),
            pltpu.VMEM((STATE, width), BF16),
            pltpu.VMEM((STATE, width), BF16),
            pltpu.VMEM((n_head, tiles, TILE), F32),
            dma((4,)),
            dma((12,)),
            dma((3,)),
            dma((3,)),
            dma((CHUNKS,)),
            dma((CHUNKS,)),
            dma((n_head - 1,)),
            dma((n_head - 1,)),
        ],
        compiler_params=pltpu.CompilerParams(
            collective_id=0, has_side_effects=True, vmem_limit_bytes=60 * 1024 * 1024
        ),
    )(
        x_in,
        bc_in,
        z_in,
        dt_in,
        conv_x_w,
        conv_x_b.reshape(1, -1),
        conv_bc_w,
        conv_bc_b.reshape(1, -1),
        dt_bias,
        a_log,
        skip_gain,
        norm_w.reshape(1, -1),
        doc_len,
    )
    return pl.pallas_call(
        scale_kernel,
        out_shape=jax.ShapeDtypeStruct((rows, width), BF16),
        in_specs=[vmem, vmem],
        out_specs=anywhere,
        scratch_shapes=[pltpu.VMEM((rows, width), BF16), dma((tiles // 2,))],
        compiler_params=pltpu.CompilerParams(vmem_limit_bytes=4 * 1024 * 1024),
    )(gated, scale)


def solution(mesh):
    return jax.shard_map(
        shards,
        mesh=mesh,
        in_specs=(
            P("context", "head"),
            P("context", None),
            P("context", "head"),
            P("head", "context"),
            P(None, "head"),
            P("head"),
            P(),
            P(),
            P("head"),
            P("head"),
            P("head"),
            P("head"),
            P(),
        ),
        out_specs=P("context", "head"),
        check_vma=False,
    )
```

```python
import functools
import math

import jax
import jax.numpy as jnp
from jax import lax
from jax.experimental import pallas as pl
from jax.experimental.pallas import tpu as pltpu
from jax.sharding import PartitionSpec as P

HEAD_DIM = 64
STATE = 256
GROUPS = 8
CONV = 4
BLOCK = 256
TILE = 128
HALO = 16
CHUNKS = 4
LOG2E = math.log2(math.e)
NORM_FLOOR = 1e-05
F32 = jnp.float32
BF16 = jnp.bfloat16


def dot(a, b, dims):
    return lax.dot_general(a, b, (dims, ((), ())), preferred_element_type=F32)


def silu_half(h):
    return h + h * jnp.tanh(h)


def split_rows(v, parts):
    pieces = []
    for _ in range(parts):
        piece = v.astype(BF16).astype(F32)
        pieces.append(piece)
        v = v - piece
    return jnp.concatenate(pieces, axis=0).astype(BF16)


def layer_kernel(
    n_ctx,
    n_head,
    x_hbm,
    bc_hbm,
    z_hbm,
    dt_hbm,
    xw_hbm,
    xb_hbm,
    bcw_hbm,
    bcb_hbm,
    dt_bias_hbm,
    a_log_hbm,
    skip_hbm,
    nw_hbm,
    doc_hbm,
    gated_ref,
    scale_ref,
    dt_ref,
    taps_buf,
    bias_buf,
    nw_ref,
    dt_bias,
    a_log,
    skip_gain,
    doc_len,
    shift_buf,
    ext,
    z_buf,
    mixed,
    tail_buf,
    entry_buf,
    state_buf,
    end_buf,
    y_buf,
    gate_buf,
    send_buf,
    recv_buf,
    sums,
    load_sems,
    small_sems,
    halo_send,
    halo_recv,
    state_send,
    state_recv,
    sums_send,
    sums_recv,
):
    rows = x_hbm.shape[0]
    width = x_hbm.shape[1]
    heads = dt_ref.shape[0]
    docs = doc_len.shape[0]
    blocks = rows // BLOCK
    tiles = rows // TILE
    ctx = lax.axis_index("context")
    me = lax.axis_index("head")
    per_group = n_head * heads // GROUPS
    group = me * heads // per_group
    b_at = pl.multiple_of(group * STATE, STATE)
    c_at = pl.multiple_of((GROUPS + group) * STATE, STATE)
    not_last = ctx < n_ctx - 1
    rounds = recv_buf.shape[0]

    barrier = pltpu.get_barrier_semaphore()

    @pl.when(ctx > 0)
    def _():
        pl.semaphore_signal(
            barrier, inc=1, device_id=(ctx - 1, me), device_id_type=pl.DeviceIdType.MESH
        )

    peers = [lax.rem(me + d, n_head) for d in range(1, n_head)]
    for peer in peers:
        pl.semaphore_signal(
            barrier, inc=1, device_id=(ctx, peer), device_id_type=pl.DeviceIdType.MESH
        )

    pairs = [
        (doc_hbm, doc_len),
        (dt_hbm, dt_ref),
        (dt_bias_hbm, dt_bias),
        (a_log_hbm, a_log),
        (skip_hbm, skip_gain),
        (xw_hbm, taps_buf.at[0]),
        (bcw_hbm.at[:, pl.ds(b_at, STATE)], taps_buf.at[1]),
        (bcw_hbm.at[:, pl.ds(c_at, STATE)], taps_buf.at[2]),
        (xb_hbm, bias_buf.at[0]),
        (bcb_hbm.at[:, pl.ds(b_at, STATE)], bias_buf.at[1]),
        (bcb_hbm.at[:, pl.ds(c_at, STATE)], bias_buf.at[2]),
        (nw_hbm, nw_ref),
    ]
    smalls = [
        pltpu.make_async_copy(src, dst, small_sems.at[i]) for i, (src, dst) in enumerate(pairs)
    ]
    for small in smalls:
        small.start()

    own = pl.ds(HALO, rows)
    loads = [
        pltpu.make_async_copy(x_hbm, ext.at[own, pl.ds(0, width)], load_sems.at[0]),
        pltpu.make_async_copy(
            bc_hbm.at[:, pl.ds(b_at, STATE)], ext.at[own, pl.ds(width, STATE)], load_sems.at[1]
        ),
        pltpu.make_async_copy(
            bc_hbm.at[:, pl.ds(c_at, STATE)],
            ext.at[own, pl.ds(width + STATE, STATE)],
            load_sems.at[2],
        ),
        pltpu.make_async_copy(z_hbm, z_buf, load_sems.at[3]),
    ]
    for load in loads:
        load.start()

    @pl.when(ctx == 0)
    def _():
        ext[pl.ds(0, HALO), :] = jnp.zeros((HALO, width + 2 * STATE), BF16)
        recv_buf[...] = jnp.zeros(recv_buf.shape, BF16)

    for small in smalls:
        small.wait()

    first = ctx * rows
    ends, begins, total = [], [], jnp.int32(0)
    for d in range(docs):
        begins.append(total)
        total = total + doc_len[d]
        ends.append(total)

    def tokens_left(pos):
        end = jnp.zeros_like(pos)
        for d in reversed(range(docs)):
            end = jnp.where(pos < ends[d], ends[d], end)
        return jnp.where(pos < 0, -1, end - 1 - pos)

    ext_lanes = rows + TILE
    left_ext = tokens_left(first - HALO + lax.broadcasted_iota(jnp.int32, (1, ext_lanes), 1))
    lane = lax.broadcasted_iota(jnp.int32, (1, rows), 1)
    pos = first + lane
    left = tokens_left(pos)
    begin = jnp.zeros_like(pos)
    for d in range(docs):
        begin = jnp.where(pos >= begins[d], begins[d], begin)
    lane_b = lax.rem(lane, BLOCK)
    alive = pos - begin > lane_b
    tail_same = left >= BLOCK - 1 - lane_b

    head_row = lax.broadcasted_iota(jnp.int32, (heads, rows), 0)
    bias_col = jnp.zeros((heads, rows), F32)
    alog_col = jnp.zeros((heads, rows), F32)
    for h in range(heads):
        bias_col = jnp.where(head_row == h, dt_bias[h], bias_col)
        alog_col = jnp.where(head_row == h, a_log[h], alog_col)
    raw = dt_ref[...].astype(F32) + bias_col
    step = jnp.maximum(raw, 0.0) + jnp.log1p(jnp.exp(-jnp.abs(raw)))
    log_decay = step * (jnp.exp(alog_col) * (-LOG2E))
    per_block = jnp.concatenate(
        [log_decay[:, c * BLOCK : (c + 1) * BLOCK] for c in range(blocks)], axis=0
    )
    upper = (
        lax.broadcasted_iota(jnp.int32, (BLOCK, BLOCK), 0)
        <= lax.broadcasted_iota(jnp.int32, (BLOCK, BLOCK), 1)
    )
    n_run = blocks * heads
    summed = dot(split_rows(per_block, 3), upper.astype(F32).astype(BF16), ((1,), (0,)))
    run = summed[:n_run] + summed[n_run : 2 * n_run] + summed[2 * n_run :]
    run_col = jnp.transpose(run)
    ends_run = run[:, BLOCK - 1 : BLOCK]
    running = jnp.concatenate([run[c * heads : (c + 1) * heads] for c in range(blocks)], axis=1)
    to_end = jnp.concatenate(
        [
            ends_run[c * heads : (c + 1) * heads] - run[c * heads : (c + 1) * heads]
            for c in range(blocks)
        ],
        axis=1,
    )
    tail_rows = jnp.where(tail_same, jnp.exp2(to_end), 0.0) * step
    entry_rows = jnp.where(alive, jnp.exp2(running), 0.0)

    spread = (
        lax.broadcasted_iota(jnp.int32, (heads, width), 0)
        == lax.broadcasted_iota(jnp.int32, (heads, width), 1) // HEAD_DIM
    ).astype(F32)
    spread2 = jnp.concatenate([spread, spread], axis=0).astype(BF16)
    tail_buf[...] = dot(split_rows(tail_rows, 2), spread2, ((0,), (0,)))

    decay_rows = []
    for c in range(blocks):
        at = c * BLOCK + BLOCK - 1
        decay_rows.append(jnp.sum(entry_rows[:, at : at + 1] * spread, axis=0, keepdims=True))
    skip_row = jnp.zeros((1, width), F32)
    head_lane = lax.broadcasted_iota(jnp.int32, (1, width), 1) // HEAD_DIM
    for h in range(heads):
        skip_row = jnp.where(head_lane == h, skip_gain[h], skip_row)

    pl.semaphore_wait(barrier, n_head - 1 + jnp.where(not_last, 1, 0))

    right = (jnp.minimum(ctx + 1, n_ctx - 1), me)
    last_rows = pl.ds(rows - HALO, HALO)
    halo_src = [
        x_hbm.at[last_rows, :],
        bc_hbm.at[last_rows, pl.ds(b_at, STATE)],
        bc_hbm.at[last_rows, pl.ds(c_at, STATE)],
    ]
    halo_at = [pl.ds(0, width), pl.ds(width, STATE), pl.ds(width + STATE, STATE)]

    def halo_copy(i):
        return pltpu.make_async_remote_copy(
            src_ref=halo_src[i],
            dst_ref=ext.at[pl.ds(0, HALO), halo_at[i]],
            send_sem=halo_send.at[i],
            recv_sem=halo_recv.at[i],
            device_id=right,
            device_id_type=pl.DeviceIdType.MESH,
        )

    @pl.when(not_last)
    def _():
        for i in range(3):
            halo_copy(i).start()

    reach = TILE + HALO
    offset = lax.broadcasted_iota(jnp.int32, (TILE, reach), 1) - lax.broadcasted_iota(
        jnp.int32, (TILE, reach), 0
    )
    bands = [jnp.where(offset == HALO - j, 1.0, 0.0).astype(F32) for j in range(1, CONV)]
    taps = [taps_buf[i] * 0.5 for i in range(3)]
    conv_bias = [bias_buf[i] * 0.5 for i in range(3)]
    part_at = [(0, width), (width, STATE), (width + STATE, STATE)]

    def conv_tile(i, parts):
        at = i * TILE
        if 0 in parts:
            ok = left_ext[:, at : at + reach]
            shift = jnp.concatenate(
                [jnp.where(ok >= j, bands[j - 1], 0.0) for j in range(1, CONV)], axis=0
            ).astype(BF16)
            shift_buf[i] = shift
        else:
            shift = shift_buf[i]
        for part in parts:
            begin_at, size = part_at[part]
            source = ext[at : at + reach, begin_at : begin_at + size]
            moved = dot(shift, source, ((1,), (0,)))
            h = conv_bias[part] + taps[part][3:4] * source[HALO:].astype(F32)
            h = h + taps[part][2:3] * moved[:TILE]
            h = h + taps[part][1:2] * moved[TILE : 2 * TILE]
            h = h + taps[part][0:1] * moved[2 * TILE :]
            mixed[at : at + TILE, begin_at : begin_at + size] = silu_half(h).astype(BF16)

    loads[0].wait()
    loads[1].wait()
    for i in range(1, tiles):
        conv_tile(i, (0, 1))

    @pl.when(ctx > 0)
    def _():
        for i in range(3):
            halo_copy(i).wait_recv()

    conv_tile(0, (0, 1))

    state = jnp.zeros((STATE, width), F32)
    for c in range(blocks):
        at = c * BLOCK
        state_buf[c] = state
        x_tail = (mixed[at : at + BLOCK, :width].astype(F32) * tail_buf[at : at + BLOCK, :]).astype(
            BF16
        )
        summary = dot(mixed[at : at + BLOCK, width : width + STATE], x_tail, ((0,), (0,)))
        state = state * decay_rows[c] + summary
    end_buf[...] = state
    shard_decay = decay_rows[0]
    for c in range(1, blocks):
        shard_decay = shard_decay * decay_rows[c]

    chunk = STATE // CHUNKS

    def state_copy(turn, i):
        at = pl.ds(i * chunk, chunk)
        return pltpu.make_async_remote_copy(
            src_ref=send_buf.at[turn, at, :],
            dst_ref=recv_buf.at[turn, at, :],
            send_sem=state_send.at[turn, i],
            recv_sem=state_recv.at[turn, i],
            device_id=right,
            device_id_type=pl.DeviceIdType.MESH,
        )

    @pl.when(not_last)
    def _():
        for i in range(CHUNKS):
            at = pl.ds(i * chunk, chunk)
            send_buf[0, at, :] = end_buf[at, :].astype(BF16)
            state_copy(0, i).start()

    def arrived(turn, chunks):
        @pl.when(ctx > 0)
        def _():
            for i in chunks:
                state_copy(turn, i).wait_recv()

    def pass_on(turn, chunks):
        for i in chunks:
            arrived(turn, [i])

            @pl.when(not_last)
            def _():
                at = pl.ds(i * chunk, chunk)
                send_buf[turn + 1, at, :] = (
                    end_buf[at, :] + shard_decay * recv_buf[turn, at, :].astype(F32)
                ).astype(BF16)
                state_copy(turn + 1, i).start()

    halves = [range(0, CHUNKS // 2), range(CHUNKS // 2, CHUNKS)]

    entry_buf[...] = dot(split_rows(entry_rows, 2), spread2, ((0,), (0,)))
    loads[2].wait()
    loads[3].wait()
    gap_at = lax.broadcasted_iota(jnp.int32, (BLOCK, BLOCK), 0) - lax.broadcasted_iota(
        jnp.int32, (BLOCK, BLOCK), 1
    )
    for c in range(blocks):
        at = c * BLOCK
        for i in range(BLOCK // TILE):
            conv_tile(c * (BLOCK // TILE) + i, (2,))
        x_c = mixed[at : at + BLOCK, :width]
        b_c = mixed[at : at + BLOCK, width : width + STATE]
        c_c = mixed[at : at + BLOCK, width + STATE :]
        inner = dot(c_c, b_c, ((1,), (1,)))
        inner = jnp.where((gap_at >= 0) & (gap_at <= left[:, at : at + BLOCK]), inner, 0.0)
        x_heads = [x_c * (head_lane == h).astype(F32).astype(BF16) for h in range(heads)]
        for lo in range(0, BLOCK, TILE):
            hi = lo + TILE
            y = skip_row * x_c[lo:hi].astype(F32)
            for h in range(heads):
                r = c * heads + h
                gap = jnp.minimum(run_col[lo:hi, r : r + 1] - run[r : r + 1, :hi], 0.0)
                mix = jnp.exp2(gap) * inner[lo:hi, :hi] * step[h : h + 1, at : at + hi]
                y = y + dot(mix.astype(BF16), x_heads[h][:hi], ((1,), (0,)))
            y_buf[at + lo : at + hi, :] = y
        if rounds > 1 and c >= blocks - 2:
            pass_on(0, halves[c - (blocks - 2)])

    for turn in range(1, rounds - 1):
        pass_on(turn, range(CHUNKS))
    for c in range(blocks):
        at = c * BLOCK
        gate_buf[at : at + BLOCK, :] = silu_half(z_buf[at : at + BLOCK, :].astype(F32) * 0.5)
        if c > 0:
            local = dot(
                mixed[at : at + BLOCK, width + STATE :], state_buf[c].astype(BF16), ((1,), (0,))
            )
            y_buf[at : at + BLOCK, :] += entry_buf[at : at + BLOCK, :] * local

    arrived(rounds - 1, range(CHUNKS))

    norm_row = nw_ref[...]
    entering = recv_buf[rounds - 1]
    so_far = jnp.ones((1, width), F32)
    ones = jnp.ones((8, width), BF16)
    slot_row = lax.broadcasted_iota(jnp.int32, (tiles, TILE), 0)
    squares = jnp.zeros((tiles, TILE), F32)
    for c in range(blocks):
        at = c * BLOCK
        from_state = dot(mixed[at : at + BLOCK, width + STATE :], entering, ((1,), (0,)))
        y = y_buf[at : at + BLOCK, :] + entry_buf[at : at + BLOCK, :] * so_far * from_state
        so_far = so_far * decay_rows[c]
        gated = y * gate_buf[at : at + BLOCK, :]
        gated_ref[at : at + BLOCK, :] = gated * norm_row
        row = dot(ones, (gated * gated).astype(BF16), ((1,), (1,)))
        for i in range(BLOCK // TILE):
            squares = jnp.where(
                slot_row == c * (BLOCK // TILE) + i, row[0:1, i * TILE : (i + 1) * TILE], squares
            )
    sums[me] = squares

    def sums_copy(d):
        return pltpu.make_async_remote_copy(
            src_ref=sums.at[me],
            dst_ref=sums.at[me],
            send_sem=sums_send.at[d],
            recv_sem=sums_recv.at[d],
            device_id=(ctx, peers[d]),
            device_id_type=pl.DeviceIdType.MESH,
        )

    for d in range(n_head - 1):
        sums_copy(d).start()
    for d in range(n_head - 1):
        sums_copy(d).wait_recv()
    every = sums[0]
    for d in range(1, n_head):
        every = every + sums[d]
    scale_ref[...] = lax.rsqrt(every / (n_head * width) + NORM_FLOOR)

    for d in range(n_head - 1):
        sums_copy(d).wait_send()

    @pl.when(not_last)
    def _():
        for i in range(3):
            halo_copy(i).wait_send()
        for turn in range(rounds):
            for i in range(CHUNKS):
                state_copy(turn, i).wait_send()


def scale_kernel(gated_ref, scale_ref, out_hbm, out_buf, out_sems):
    rows, width = gated_ref.shape
    stores = []
    for t in range(rows // TILE):
        at = pl.ds(t * TILE, TILE)
        column = jnp.transpose(jnp.broadcast_to(scale_ref[t : t + 1, :], (TILE, TILE)))
        column = jnp.concatenate([column] * (width // TILE), axis=1)
        out_buf[at, :] = (gated_ref[at, :] * column).astype(BF16)
        if t % 2 == 1:
            pair = pl.ds((t - 1) * TILE, 2 * TILE)
            store = pltpu.make_async_copy(
                out_buf.at[pair, :], out_hbm.at[pair, :], out_sems.at[t // 2]
            )
            store.start()
            stores.append(store)
    for store in stores:
        store.wait()


def shards(
    x_in,
    bc_in,
    z_in,
    dt_in,
    conv_x_w,
    conv_x_b,
    conv_bc_w,
    conv_bc_b,
    dt_bias,
    a_log,
    skip_gain,
    norm_w,
    doc_len,
):
    rows, width = x_in.shape
    n_ctx = lax.axis_size("context")
    n_head = lax.axis_size("head")
    rounds = max(1, n_ctx // 2)
    blocks = rows // BLOCK
    tiles = rows // TILE
    anywhere = pl.BlockSpec(memory_space=pltpu.HBM)
    heads = dt_in.shape[0]
    docs = doc_len.shape[0]
    vmem = pl.BlockSpec(memory_space=pltpu.VMEM)
    dma = pltpu.SemaphoreType.DMA
    gated, scale = pl.pallas_call(
        functools.partial(layer_kernel, n_ctx, n_head),
        out_shape=(pltpu.VMEM((rows, width), F32), pltpu.VMEM((tiles, TILE), F32)),
        in_specs=[anywhere] * 13,
        out_specs=(vmem, vmem),
        scratch_shapes=[
            pltpu.VMEM((heads, rows), BF16),
            pltpu.VMEM((3, CONV, width), F32),
            pltpu.VMEM((3, 1, width), F32),
            pltpu.VMEM((1, width), F32),
            pltpu.SMEM((heads,), F32),
            pltpu.SMEM((heads,), F32),
            pltpu.SMEM((heads,), F32),
            pltpu.SMEM((docs,), jnp.int32),
            pltpu.VMEM((tiles, (CONV - 1) * TILE, TILE + HALO), BF16),
            pltpu.VMEM((rows + HALO, width + 2 * STATE), BF16),
            pltpu.VMEM((rows, width), BF16),
            pltpu.VMEM((rows, width + 2 * STATE), BF16),
            pltpu.VMEM((rows, width), F32),
            pltpu.VMEM((rows, width), F32),
            pltpu.VMEM((blocks, STATE, width), F32),
            pltpu.VMEM((STATE, width), F32),
            pltpu.VMEM((rows, width), F32),
            pltpu.VMEM((rows, width), F32),
            pltpu.VMEM((rounds, STATE, width), BF16),
            pltpu.VMEM((rounds, STATE, width), BF16),
            pltpu.VMEM((n_head, tiles, TILE), F32),
            dma((4,)),
            dma((12,)),
            dma((3,)),
            dma((3,)),
            dma((rounds, CHUNKS)),
            dma((rounds, CHUNKS)),
            dma((n_head - 1,)),
            dma((n_head - 1,)),
        ],
        compiler_params=pltpu.CompilerParams(
            collective_id=0, has_side_effects=True, vmem_limit_bytes=60 * 1024 * 1024
        ),
    )(
        x_in,
        bc_in,
        z_in,
        dt_in,
        conv_x_w,
        conv_x_b.reshape(1, -1),
        conv_bc_w,
        conv_bc_b.reshape(1, -1),
        dt_bias,
        a_log,
        skip_gain,
        norm_w.reshape(1, -1),
        doc_len,
    )
    return pl.pallas_call(
        scale_kernel,
        out_shape=jax.ShapeDtypeStruct((rows, width), BF16),
        in_specs=[vmem, vmem],
        out_specs=anywhere,
        scratch_shapes=[pltpu.VMEM((rows, width), BF16), dma((tiles // 2,))],
        compiler_params=pltpu.CompilerParams(vmem_limit_bytes=4 * 1024 * 1024),
    )(gated, scale)


def solution(mesh):
    return jax.shard_map(
        shards,
        mesh=mesh,
        in_specs=(
            P("context", "head"),
            P("context", None),
            P("context", "head"),
            P("head", "context"),
            P(None, "head"),
            P("head"),
            P(),
            P(),
            P("head"),
            P("head"),
            P("head"),
            P("head"),
            P(),
        ),
        out_specs=P("context", "head"),
        check_vma=False,
    )
```

```python
import functools
import math

import jax
import jax.numpy as jnp
from jax import lax
from jax.experimental import pallas as pl
from jax.experimental.pallas import tpu as pltpu
from jax.sharding import PartitionSpec as P

HEAD_DIM = 64
STATE = 256
GROUPS = 8
CONV = 4
BLOCK = 256
TILE = 128
HALO = 16
CHUNKS = 8
LOG2E = math.log2(math.e)
NORM_FLOOR = 1e-05
F32 = jnp.float32
BF16 = jnp.bfloat16


def dot(a, b, dims):
    return lax.dot_general(a, b, (dims, ((), ())), preferred_element_type=F32)


def silu_half(h):
    return h + h * jnp.tanh(h)


def split_rows(v, parts):
    pieces = []
    for _ in range(parts):
        piece = v.astype(BF16).astype(F32)
        pieces.append(piece)
        v = v - piece
    return jnp.concatenate(pieces, axis=0).astype(BF16)


def layer_kernel(
    n_ctx,
    n_head,
    x_hbm,
    bc_hbm,
    z_hbm,
    dt_hbm,
    xw_hbm,
    xb_hbm,
    bcw_hbm,
    bcb_hbm,
    dt_bias_hbm,
    a_log_hbm,
    skip_hbm,
    nw_hbm,
    doc_hbm,
    gated_ref,
    scale_ref,
    dt_ref,
    taps_buf,
    bias_buf,
    nw_ref,
    dt_bias,
    a_log,
    skip_gain,
    doc_len,
    shift_buf,
    ext,
    z_buf,
    mixed,
    tail_buf,
    entry_buf,
    state_buf,
    end_buf,
    y_buf,
    gate_buf,
    send_buf,
    recv_buf,
    x_tail_buf,
    sums,
    load_sems,
    small_sems,
    halo_send,
    halo_recv,
    state_send,
    state_recv,
    sums_send,
    sums_recv,
):
    rows = x_hbm.shape[0]
    width = x_hbm.shape[1]
    heads = dt_ref.shape[0]
    docs = doc_len.shape[0]
    blocks = rows // BLOCK
    tiles = rows // TILE
    ctx = lax.axis_index("context")
    me = lax.axis_index("head")
    per_group = n_head * heads // GROUPS
    group = me * heads // per_group
    b_at = pl.multiple_of(group * STATE, STATE)
    c_at = pl.multiple_of((GROUPS + group) * STATE, STATE)
    not_last = ctx < n_ctx - 1

    barrier = pltpu.get_barrier_semaphore()

    @pl.when(ctx > 0)
    def _():
        pl.semaphore_signal(
            barrier, inc=1, device_id=(ctx - 1, me), device_id_type=pl.DeviceIdType.MESH
        )

    peers = [lax.rem(me + d, n_head) for d in range(1, n_head)]
    for peer in peers:
        pl.semaphore_signal(
            barrier, inc=1, device_id=(ctx, peer), device_id_type=pl.DeviceIdType.MESH
        )

    pairs = [
        (doc_hbm, doc_len),
        (dt_hbm, dt_ref),
        (dt_bias_hbm, dt_bias),
        (a_log_hbm, a_log),
        (skip_hbm, skip_gain),
        (xw_hbm, taps_buf.at[0]),
        (bcw_hbm.at[:, pl.ds(b_at, STATE)], taps_buf.at[1]),
        (bcw_hbm.at[:, pl.ds(c_at, STATE)], taps_buf.at[2]),
        (xb_hbm, bias_buf.at[0]),
        (bcb_hbm.at[:, pl.ds(b_at, STATE)], bias_buf.at[1]),
        (bcb_hbm.at[:, pl.ds(c_at, STATE)], bias_buf.at[2]),
        (nw_hbm, nw_ref),
    ]
    smalls = [
        pltpu.make_async_copy(src, dst, small_sems.at[i]) for i, (src, dst) in enumerate(pairs)
    ]
    for small in smalls:
        small.start()

    own = pl.ds(HALO, rows)
    loads = [
        pltpu.make_async_copy(x_hbm, ext.at[own, pl.ds(0, width)], load_sems.at[0]),
        pltpu.make_async_copy(
            bc_hbm.at[:, pl.ds(b_at, STATE)], ext.at[own, pl.ds(width, STATE)], load_sems.at[1]
        ),
        pltpu.make_async_copy(
            bc_hbm.at[:, pl.ds(c_at, STATE)],
            ext.at[own, pl.ds(width + STATE, STATE)],
            load_sems.at[2],
        ),
        pltpu.make_async_copy(z_hbm, z_buf, load_sems.at[3]),
    ]
    for load in loads:
        load.start()

    @pl.when(ctx == 0)
    def _():
        ext[pl.ds(0, HALO), :] = jnp.zeros((HALO, width + 2 * STATE), BF16)
        recv_buf[...] = jnp.zeros((STATE, width), BF16)

    for small in smalls:
        small.wait()

    first = ctx * rows
    ends, begins, total = [], [], jnp.int32(0)
    for d in range(docs):
        begins.append(total)
        total = total + doc_len[d]
        ends.append(total)

    def tokens_left(pos):
        end = jnp.zeros_like(pos)
        for d in reversed(range(docs)):
            end = jnp.where(pos < ends[d], ends[d], end)
        return jnp.where(pos < 0, -1, end - 1 - pos)

    ext_lanes = rows + TILE
    left_ext = tokens_left(first - HALO + lax.broadcasted_iota(jnp.int32, (1, ext_lanes), 1))
    lane = lax.broadcasted_iota(jnp.int32, (1, rows), 1)
    pos = first + lane
    left = tokens_left(pos)
    begin = jnp.zeros_like(pos)
    for d in range(docs):
        begin = jnp.where(pos >= begins[d], begins[d], begin)
    lane_b = lax.rem(lane, BLOCK)
    alive = pos - begin > lane_b
    tail_same = left >= BLOCK - 1 - lane_b

    head_row = lax.broadcasted_iota(jnp.int32, (heads, rows), 0)
    bias_col = jnp.zeros((heads, rows), F32)
    alog_col = jnp.zeros((heads, rows), F32)
    for h in range(heads):
        bias_col = jnp.where(head_row == h, dt_bias[h], bias_col)
        alog_col = jnp.where(head_row == h, a_log[h], alog_col)
    raw = dt_ref[...].astype(F32) + bias_col
    step = jnp.maximum(raw, 0.0) + jnp.log1p(jnp.exp(-jnp.abs(raw)))
    log_decay = step * (jnp.exp(alog_col) * (-LOG2E))
    per_block = jnp.concatenate(
        [log_decay[:, c * BLOCK : (c + 1) * BLOCK] for c in range(blocks)], axis=0
    )
    upper = (
        lax.broadcasted_iota(jnp.int32, (BLOCK, BLOCK), 0)
        <= lax.broadcasted_iota(jnp.int32, (BLOCK, BLOCK), 1)
    )
    n_run = blocks * heads
    summed = dot(split_rows(per_block, 3), upper.astype(F32).astype(BF16), ((1,), (0,)))
    run = summed[:n_run] + summed[n_run : 2 * n_run] + summed[2 * n_run :]
    run_col = jnp.transpose(run)
    ends_run = run[:, BLOCK - 1 : BLOCK]
    running = jnp.concatenate([run[c * heads : (c + 1) * heads] for c in range(blocks)], axis=1)
    to_end = jnp.concatenate(
        [
            ends_run[c * heads : (c + 1) * heads] - run[c * heads : (c + 1) * heads]
            for c in range(blocks)
        ],
        axis=1,
    )
    tail_rows = jnp.where(tail_same, jnp.exp2(to_end), 0.0) * step
    entry_rows = jnp.where(alive, jnp.exp2(running), 0.0)

    spread = (
        lax.broadcasted_iota(jnp.int32, (heads, width), 0)
        == lax.broadcasted_iota(jnp.int32, (heads, width), 1) // HEAD_DIM
    ).astype(F32)
    spread2 = jnp.concatenate([spread, spread], axis=0).astype(BF16)
    tail_buf[...] = dot(split_rows(tail_rows, 2), spread2, ((0,), (0,)))

    decay_rows = []
    for c in range(blocks):
        at = c * BLOCK + BLOCK - 1
        decay_rows.append(jnp.sum(entry_rows[:, at : at + 1] * spread, axis=0, keepdims=True))
    skip_row = jnp.zeros((1, width), F32)
    head_lane = lax.broadcasted_iota(jnp.int32, (1, width), 1) // HEAD_DIM
    for h in range(heads):
        skip_row = jnp.where(head_lane == h, skip_gain[h], skip_row)

    pl.semaphore_wait(barrier, n_head - 1 + jnp.where(not_last, 1, 0))

    right = (jnp.minimum(ctx + 1, n_ctx - 1), me)
    last_rows = pl.ds(rows - HALO, HALO)
    halo_src = [
        x_hbm.at[last_rows, :],
        bc_hbm.at[last_rows, pl.ds(b_at, STATE)],
        bc_hbm.at[last_rows, pl.ds(c_at, STATE)],
    ]
    halo_at = [pl.ds(0, width), pl.ds(width, STATE), pl.ds(width + STATE, STATE)]

    def halo_copy(i):
        return pltpu.make_async_remote_copy(
            src_ref=halo_src[i],
            dst_ref=ext.at[pl.ds(0, HALO), halo_at[i]],
            send_sem=halo_send.at[i],
            recv_sem=halo_recv.at[i],
            device_id=right,
            device_id_type=pl.DeviceIdType.MESH,
        )

    @pl.when(not_last)
    def _():
        for i in range(3):
            halo_copy(i).start()

    reach = TILE + HALO
    offset = lax.broadcasted_iota(jnp.int32, (TILE, reach), 1) - lax.broadcasted_iota(
        jnp.int32, (TILE, reach), 0
    )
    bands = [jnp.where(offset == HALO - j, 1.0, 0.0).astype(F32) for j in range(1, CONV)]
    taps_in = [taps_buf[i] * 0.5 for i in range(3)]
    bias_in = [bias_buf[i] * 0.5 for i in range(3)]
    part_half = STATE // 2
    taps = [taps_in[0], taps_in[1][:, :part_half], taps_in[1][:, part_half:], taps_in[2]]
    conv_bias = [bias_in[0], bias_in[1][:, :part_half], bias_in[1][:, part_half:], bias_in[2]]
    part_at = [
        (0, width),
        (width, part_half),
        (width + part_half, part_half),
        (width + STATE, STATE),
    ]

    def conv_tile(i, parts):
        at = i * TILE
        if 0 in parts:
            ok = left_ext[:, at : at + reach]
            shift = jnp.concatenate(
                [jnp.where(ok >= j, bands[j - 1], 0.0) for j in range(1, CONV)], axis=0
            ).astype(BF16)
            shift_buf[i] = shift
        else:
            shift = shift_buf[i]
        for part in parts:
            begin_at, size = part_at[part]
            source = ext[at : at + reach, begin_at : begin_at + size]
            moved = dot(shift, source, ((1,), (0,)))
            h = conv_bias[part] + taps[part][3:4] * source[HALO:].astype(F32)
            h = h + taps[part][2:3] * moved[:TILE]
            h = h + taps[part][1:2] * moved[TILE : 2 * TILE]
            h = h + taps[part][0:1] * moved[2 * TILE :]
            mixed[at : at + TILE, begin_at : begin_at + size] = silu_half(h).astype(BF16)

    loads[0].wait()
    loads[1].wait()
    for i in range(1, tiles):
        conv_tile(i, (0, 1))

    @pl.when(ctx > 0)
    def _():
        for i in range(3):
            halo_copy(i).wait_recv()

    conv_tile(0, (0, 1))

    shard_decay = decay_rows[0]
    for c in range(1, blocks):
        shard_decay = shard_decay * decay_rows[c]
    chunk = STATE // CHUNKS

    def state_copy(i):
        at = pl.ds(i * chunk, chunk)
        return pltpu.make_async_remote_copy(
            src_ref=send_buf.at[at, :],
            dst_ref=recv_buf.at[at, :],
            send_sem=state_send.at[i],
            recv_sem=state_recv.at[i],
            device_id=right,
            device_id_type=pl.DeviceIdType.MESH,
        )

    def half_states(half):
        columns = slice(half * part_half, (half + 1) * part_half)
        state = jnp.zeros((part_half, width), F32)
        for c in range(blocks):
            block = slice(c * BLOCK, (c + 1) * BLOCK)
            state_buf[c, columns, :] = state
            if half == 0:
                x_tail_buf[block, :] = (
                    mixed[block, :width].astype(F32) * tail_buf[block, :]
                ).astype(BF16)
            b_half = mixed[block, width + columns.start : width + columns.stop]
            state = state * decay_rows[c] + dot(b_half, x_tail_buf[block, :], ((0,), (0,)))
        end_buf[columns, :] = state

        @pl.when((ctx == 0) & not_last)
        def _():
            send_buf[columns, :] = end_buf[columns, :].astype(BF16)
            for i in range(half * CHUNKS // 2, (half + 1) * CHUNKS // 2):
                state_copy(i).start()

    half_states(0)
    for i in range(tiles):
        conv_tile(i, (2,))
    half_states(1)

    def pass_on(turn, chunks):
        if not chunks:
            return

        @pl.when(turn & not_last)
        def _():
            for i in chunks:
                at = pl.ds(i * chunk, chunk)
                state_copy(i).wait_recv()
                send_buf[at, :] = (
                    end_buf[at, :] + shard_decay * recv_buf[at, :].astype(F32)
                ).astype(BF16)
                state_copy(i).start()

    entry_buf[...] = dot(split_rows(entry_rows, 2), spread2, ((0,), (0,)))
    loads[2].wait()
    loads[3].wait()
    gap_at = lax.broadcasted_iota(jnp.int32, (BLOCK, BLOCK), 0) - lax.broadcasted_iota(
        jnp.int32, (BLOCK, BLOCK), 1
    )
    for c in range(blocks):
        at = c * BLOCK
        for i in range(BLOCK // TILE):
            conv_tile(c * (BLOCK // TILE) + i, (3,))
        x_c = mixed[at : at + BLOCK, :width]
        b_c = mixed[at : at + BLOCK, width : width + STATE]
        c_c = mixed[at : at + BLOCK, width + STATE :]
        inner = dot(c_c, b_c, ((1,), (1,)))
        inner = jnp.where((gap_at >= 0) & (gap_at <= left[:, at : at + BLOCK]), inner, 0.0)
        x_heads = [x_c * (head_lane == h).astype(F32).astype(BF16) for h in range(heads)]
        for lo in range(0, BLOCK, TILE):
            hi = lo + TILE
            y = skip_row * x_c[lo:hi].astype(F32)
            for h in range(heads):
                r = c * heads + h
                gap = jnp.minimum(run_col[lo:hi, r : r + 1] - run[r : r + 1, :hi], 0.0)
                mix = jnp.exp2(gap) * inner[lo:hi, :hi] * step[h : h + 1, at : at + hi]
                y = y + dot(mix.astype(BF16), x_heads[h][:hi], ((1,), (0,)))
            y_buf[at + lo : at + hi, :] = y
            done = c * (BLOCK // TILE) + lo // TILE
            pass_on(ctx == 1, [done] if done < CHUNKS else [])
            pass_on(ctx == 2, [done - 2] if 2 <= done < CHUNKS + 2 else [])

    pass_on(ctx == 1, list(range(tiles, CHUNKS)))
    pass_on(ctx == 2, list(range(tiles - 2, CHUNKS)))
    pass_on(ctx >= 3, list(range(CHUNKS)))
    for c in range(blocks):
        at = c * BLOCK
        gate_buf[at : at + BLOCK, :] = silu_half(z_buf[at : at + BLOCK, :].astype(F32) * 0.5)
        if c > 0:
            local = dot(
                mixed[at : at + BLOCK, width + STATE :], state_buf[c].astype(BF16), ((1,), (0,))
            )
            y_buf[at : at + BLOCK, :] += entry_buf[at : at + BLOCK, :] * local

    @pl.when((ctx > 0) & (ctx == n_ctx - 1))
    def _():
        for i in range(CHUNKS):
            state_copy(i).wait_recv()

    norm_row = nw_ref[...]
    entering = recv_buf[...]
    so_far = jnp.ones((1, width), F32)
    ones = jnp.ones((8, width), BF16)
    slot_row = lax.broadcasted_iota(jnp.int32, (tiles, TILE), 0)
    squares = jnp.zeros((tiles, TILE), F32)
    for c in range(blocks):
        at = c * BLOCK
        from_state = dot(mixed[at : at + BLOCK, width + STATE :], entering, ((1,), (0,)))
        y = y_buf[at : at + BLOCK, :] + entry_buf[at : at + BLOCK, :] * so_far * from_state
        so_far = so_far * decay_rows[c]
        gated = y * gate_buf[at : at + BLOCK, :]
        gated_ref[at : at + BLOCK, :] = gated * norm_row
        row = dot(ones, (gated * gated).astype(BF16), ((1,), (1,)))
        for i in range(BLOCK // TILE):
            squares = jnp.where(
                slot_row == c * (BLOCK // TILE) + i, row[0:1, i * TILE : (i + 1) * TILE], squares
            )
    sums[me] = squares

    def sums_copy(d):
        return pltpu.make_async_remote_copy(
            src_ref=sums.at[me],
            dst_ref=sums.at[me],
            send_sem=sums_send.at[d],
            recv_sem=sums_recv.at[d],
            device_id=(ctx, peers[d]),
            device_id_type=pl.DeviceIdType.MESH,
        )

    for d in range(n_head - 1):
        sums_copy(d).start()
    for d in range(n_head - 1):
        sums_copy(d).wait_recv()
    every = sums[0]
    for d in range(1, n_head):
        every = every + sums[d]
    scale_ref[...] = lax.rsqrt(every / (n_head * width) + NORM_FLOOR)

    for d in range(n_head - 1):
        sums_copy(d).wait_send()

    @pl.when(not_last)
    def _():
        for i in range(3):
            halo_copy(i).wait_send()
        for i in range(CHUNKS):
            state_copy(i).wait_send()


def scale_kernel(gated_ref, scale_ref, out_hbm, out_buf, out_sems):
    rows, width = gated_ref.shape
    stores = []
    for t in range(rows // TILE):
        at = pl.ds(t * TILE, TILE)
        column = jnp.transpose(jnp.broadcast_to(scale_ref[t : t + 1, :], (TILE, TILE)))
        column = jnp.concatenate([column] * (width // TILE), axis=1)
        out_buf[at, :] = (gated_ref[at, :] * column).astype(BF16)
        if t % 2 == 1:
            pair = pl.ds((t - 1) * TILE, 2 * TILE)
            store = pltpu.make_async_copy(
                out_buf.at[pair, :], out_hbm.at[pair, :], out_sems.at[t // 2]
            )
            store.start()
            stores.append(store)
    for store in stores:
        store.wait()


def shards(
    x_in,
    bc_in,
    z_in,
    dt_in,
    conv_x_w,
    conv_x_b,
    conv_bc_w,
    conv_bc_b,
    dt_bias,
    a_log,
    skip_gain,
    norm_w,
    doc_len,
):
    rows, width = x_in.shape
    n_ctx = lax.axis_size("context")
    n_head = lax.axis_size("head")
    blocks = rows // BLOCK
    tiles = rows // TILE
    anywhere = pl.BlockSpec(memory_space=pltpu.HBM)
    heads = dt_in.shape[0]
    docs = doc_len.shape[0]
    vmem = pl.BlockSpec(memory_space=pltpu.VMEM)
    dma = pltpu.SemaphoreType.DMA
    gated, scale = pl.pallas_call(
        functools.partial(layer_kernel, n_ctx, n_head),
        out_shape=(pltpu.VMEM((rows, width), F32), pltpu.VMEM((tiles, TILE), F32)),
        in_specs=[anywhere] * 13,
        out_specs=(vmem, vmem),
        scratch_shapes=[
            pltpu.VMEM((heads, rows), BF16),
            pltpu.VMEM((3, CONV, width), F32),
            pltpu.VMEM((3, 1, width), F32),
            pltpu.VMEM((1, width), F32),
            pltpu.SMEM((heads,), F32),
            pltpu.SMEM((heads,), F32),
            pltpu.SMEM((heads,), F32),
            pltpu.SMEM((docs,), jnp.int32),
            pltpu.VMEM((tiles, (CONV - 1) * TILE, TILE + HALO), BF16),
            pltpu.VMEM((rows + HALO, width + 2 * STATE), BF16),
            pltpu.VMEM((rows, width), BF16),
            pltpu.VMEM((rows, width + 2 * STATE), BF16),
            pltpu.VMEM((rows, width), F32),
            pltpu.VMEM((rows, width), F32),
            pltpu.VMEM((blocks, STATE, width), F32),
            pltpu.VMEM((STATE, width), F32),
            pltpu.VMEM((rows, width), F32),
            pltpu.VMEM((rows, width), F32),
            pltpu.VMEM((STATE, width), BF16),
            pltpu.VMEM((STATE, width), BF16),
            pltpu.VMEM((rows, width), BF16),
            pltpu.VMEM((n_head, tiles, TILE), F32),
            dma((4,)),
            dma((12,)),
            dma((3,)),
            dma((3,)),
            dma((CHUNKS,)),
            dma((CHUNKS,)),
            dma((n_head - 1,)),
            dma((n_head - 1,)),
        ],
        compiler_params=pltpu.CompilerParams(
            collective_id=0, has_side_effects=True, vmem_limit_bytes=60 * 1024 * 1024
        ),
    )(
        x_in,
        bc_in,
        z_in,
        dt_in,
        conv_x_w,
        conv_x_b.reshape(1, -1),
        conv_bc_w,
        conv_bc_b.reshape(1, -1),
        dt_bias,
        a_log,
        skip_gain,
        norm_w.reshape(1, -1),
        doc_len,
    )
    return pl.pallas_call(
        scale_kernel,
        out_shape=jax.ShapeDtypeStruct((rows, width), BF16),
        in_specs=[vmem, vmem],
        out_specs=anywhere,
        scratch_shapes=[pltpu.VMEM((rows, width), BF16), dma((tiles // 2,))],
        compiler_params=pltpu.CompilerParams(vmem_limit_bytes=4 * 1024 * 1024),
    )(gated, scale)


def solution(mesh):
    return jax.shard_map(
        shards,
        mesh=mesh,
        in_specs=(
            P("context", "head"),
            P("context", None),
            P("context", "head"),
            P("head", "context"),
            P(None, "head"),
            P("head"),
            P(),
            P(),
            P("head"),
            P("head"),
            P("head"),
            P("head"),
            P(),
        ),
        out_specs=P("context", "head"),
        check_vma=False,
    )
```

```python
import functools
import math

import jax
import jax.numpy as jnp
from jax import lax
from jax.experimental import pallas as pl
from jax.experimental.pallas import tpu as pltpu
from jax.sharding import PartitionSpec as P

HEAD_DIM = 64
STATE = 256
GROUPS = 8
CONV = 4
BLOCK = 256
TILE = 128
HALO = 16
CHUNKS = 8
LOG2E = math.log2(math.e)
NORM_FLOOR = 1e-05
F32 = jnp.float32
BF16 = jnp.bfloat16


def dot(a, b, dims):
    return lax.dot_general(a, b, (dims, ((), ())), preferred_element_type=F32)


def silu_half(h):
    return h + h * jnp.tanh(h)


def split_rows(v, parts):
    pieces = []
    for _ in range(parts):
        piece = v.astype(BF16).astype(F32)
        pieces.append(piece)
        v = v - piece
    return jnp.concatenate(pieces, axis=0).astype(BF16)


def layer_kernel(
    n_ctx,
    n_head,
    x_hbm,
    bc_hbm,
    z_hbm,
    dt_hbm,
    xw_hbm,
    xb_hbm,
    bcw_hbm,
    bcb_hbm,
    dt_bias_hbm,
    a_log_hbm,
    skip_hbm,
    nw_hbm,
    doc_hbm,
    gated_ref,
    scale_ref,
    dt_ref,
    taps_buf,
    bias_buf,
    nw_ref,
    dt_bias,
    a_log,
    skip_gain,
    doc_len,
    shift_buf,
    ext,
    z_buf,
    mixed,
    tail_buf,
    entry_buf,
    state_buf,
    end_buf,
    y_buf,
    gate_buf,
    send_buf,
    recv_buf,
    sums,
    load_sems,
    small_sems,
    halo_send,
    halo_recv,
    state_send,
    state_recv,
    sums_send,
    sums_recv,
):
    rows = x_hbm.shape[0]
    width = x_hbm.shape[1]
    heads = dt_ref.shape[0]
    docs = doc_len.shape[0]
    blocks = rows // BLOCK
    tiles = rows // TILE
    ctx = lax.axis_index("context")
    me = lax.axis_index("head")
    per_group = n_head * heads // GROUPS
    group = me * heads // per_group
    b_at = pl.multiple_of(group * STATE, STATE)
    c_at = pl.multiple_of((GROUPS + group) * STATE, STATE)
    not_last = ctx < n_ctx - 1

    barrier = pltpu.get_barrier_semaphore()

    @pl.when(ctx > 0)
    def _():
        pl.semaphore_signal(
            barrier, inc=1, device_id=(ctx - 1, me), device_id_type=pl.DeviceIdType.MESH
        )

    peers = [lax.rem(me + d, n_head) for d in range(1, n_head)]
    for peer in peers:
        pl.semaphore_signal(
            barrier, inc=1, device_id=(ctx, peer), device_id_type=pl.DeviceIdType.MESH
        )

    pairs = [
        (doc_hbm, doc_len),
        (dt_hbm, dt_ref),
        (dt_bias_hbm, dt_bias),
        (a_log_hbm, a_log),
        (skip_hbm, skip_gain),
        (xw_hbm, taps_buf.at[0]),
        (bcw_hbm.at[:, pl.ds(b_at, STATE)], taps_buf.at[1]),
        (bcw_hbm.at[:, pl.ds(c_at, STATE)], taps_buf.at[2]),
        (xb_hbm, bias_buf.at[0]),
        (bcb_hbm.at[:, pl.ds(b_at, STATE)], bias_buf.at[1]),
        (bcb_hbm.at[:, pl.ds(c_at, STATE)], bias_buf.at[2]),
        (nw_hbm, nw_ref),
    ]
    smalls = [
        pltpu.make_async_copy(src, dst, small_sems.at[i]) for i, (src, dst) in enumerate(pairs)
    ]
    for small in smalls:
        small.start()

    own = pl.ds(HALO, rows)
    loads = [
        pltpu.make_async_copy(x_hbm, ext.at[own, pl.ds(0, width)], load_sems.at[0]),
        pltpu.make_async_copy(
            bc_hbm.at[:, pl.ds(b_at, STATE)], ext.at[own, pl.ds(width, STATE)], load_sems.at[1]
        ),
        pltpu.make_async_copy(
            bc_hbm.at[:, pl.ds(c_at, STATE)],
            ext.at[own, pl.ds(width + STATE, STATE)],
            load_sems.at[2],
        ),
        pltpu.make_async_copy(z_hbm, z_buf, load_sems.at[3]),
    ]
    for load in loads:
        load.start()

    @pl.when(ctx == 0)
    def _():
        ext[pl.ds(0, HALO), :] = jnp.zeros((HALO, width + 2 * STATE), BF16)
        recv_buf[...] = jnp.zeros((STATE, width), BF16)

    for small in smalls:
        small.wait()

    first = ctx * rows
    ends, begins, total = [], [], jnp.int32(0)
    for d in range(docs):
        begins.append(total)
        total = total + doc_len[d]
        ends.append(total)

    def tokens_left(pos):
        end = jnp.zeros_like(pos)
        for d in reversed(range(docs)):
            end = jnp.where(pos < ends[d], ends[d], end)
        return jnp.where(pos < 0, -1, end - 1 - pos)

    ext_lanes = rows + TILE
    left_ext = tokens_left(first - HALO + lax.broadcasted_iota(jnp.int32, (1, ext_lanes), 1))
    lane = lax.broadcasted_iota(jnp.int32, (1, rows), 1)
    pos = first + lane
    left = tokens_left(pos)
    begin = jnp.zeros_like(pos)
    for d in range(docs):
        begin = jnp.where(pos >= begins[d], begins[d], begin)
    lane_b = lax.rem(lane, BLOCK)
    alive = pos - begin > lane_b
    tail_same = left >= BLOCK - 1 - lane_b

    head_row = lax.broadcasted_iota(jnp.int32, (heads, rows), 0)
    bias_col = jnp.zeros((heads, rows), F32)
    alog_col = jnp.zeros((heads, rows), F32)
    for h in range(heads):
        bias_col = jnp.where(head_row == h, dt_bias[h], bias_col)
        alog_col = jnp.where(head_row == h, a_log[h], alog_col)
    raw = dt_ref[...].astype(F32) + bias_col
    step = jnp.maximum(raw, 0.0) + jnp.log1p(jnp.exp(-jnp.abs(raw)))
    log_decay = step * (jnp.exp(alog_col) * (-LOG2E))
    per_block = jnp.concatenate(
        [log_decay[:, c * BLOCK : (c + 1) * BLOCK] for c in range(blocks)], axis=0
    )
    upper = (
        lax.broadcasted_iota(jnp.int32, (BLOCK, BLOCK), 0)
        <= lax.broadcasted_iota(jnp.int32, (BLOCK, BLOCK), 1)
    )
    n_run = blocks * heads
    summed = dot(split_rows(per_block, 3), upper.astype(F32).astype(BF16), ((1,), (0,)))
    run = summed[:n_run] + summed[n_run : 2 * n_run] + summed[2 * n_run :]
    run_col = jnp.transpose(run)
    ends_run = run[:, BLOCK - 1 : BLOCK]
    running = jnp.concatenate([run[c * heads : (c + 1) * heads] for c in range(blocks)], axis=1)
    to_end = jnp.concatenate(
        [
            ends_run[c * heads : (c + 1) * heads] - run[c * heads : (c + 1) * heads]
            for c in range(blocks)
        ],
        axis=1,
    )
    tail_rows = jnp.where(tail_same, jnp.exp2(to_end), 0.0) * step
    entry_rows = jnp.where(alive, jnp.exp2(running), 0.0)

    spread = (
        lax.broadcasted_iota(jnp.int32, (heads, width), 0)
        == lax.broadcasted_iota(jnp.int32, (heads, width), 1) // HEAD_DIM
    ).astype(F32)
    spread2 = jnp.concatenate([spread, spread], axis=0).astype(BF16)
    tail_buf[...] = dot(split_rows(tail_rows, 2), spread2, ((0,), (0,)))

    decay_rows = []
    for c in range(blocks):
        at = c * BLOCK + BLOCK - 1
        decay_rows.append(jnp.sum(entry_rows[:, at : at + 1] * spread, axis=0, keepdims=True))
    skip_row = jnp.zeros((1, width), F32)
    head_lane = lax.broadcasted_iota(jnp.int32, (1, width), 1) // HEAD_DIM
    for h in range(heads):
        skip_row = jnp.where(head_lane == h, skip_gain[h], skip_row)

    pl.semaphore_wait(barrier, n_head - 1 + jnp.where(not_last, 1, 0))

    right = (jnp.minimum(ctx + 1, n_ctx - 1), me)
    last_rows = pl.ds(rows - HALO, HALO)
    halo_src = [
        x_hbm.at[last_rows, :],
        bc_hbm.at[last_rows, pl.ds(b_at, STATE)],
        bc_hbm.at[last_rows, pl.ds(c_at, STATE)],
    ]
    halo_at = [pl.ds(0, width), pl.ds(width, STATE), pl.ds(width + STATE, STATE)]

    def halo_copy(i):
        return pltpu.make_async_remote_copy(
            src_ref=halo_src[i],
            dst_ref=ext.at[pl.ds(0, HALO), halo_at[i]],
            send_sem=halo_send.at[i],
            recv_sem=halo_recv.at[i],
            device_id=right,
            device_id_type=pl.DeviceIdType.MESH,
        )

    @pl.when(not_last)
    def _():
        for i in range(3):
            halo_copy(i).start()

    reach = TILE + HALO
    offset = lax.broadcasted_iota(jnp.int32, (TILE, reach), 1) - lax.broadcasted_iota(
        jnp.int32, (TILE, reach), 0
    )
    bands = [jnp.where(offset == HALO - j, 1.0, 0.0).astype(F32) for j in range(1, CONV)]
    taps = [taps_buf[i] * 0.5 for i in range(3)]
    conv_bias = [bias_buf[i] * 0.5 for i in range(3)]
    part_at = [(0, width), (width, STATE), (width + STATE, STATE)]

    def conv_tile(i, parts):
        at = i * TILE
        if 0 in parts:
            ok = left_ext[:, at : at + reach]
            shift = jnp.concatenate(
                [jnp.where(ok >= j, bands[j - 1], 0.0) for j in range(1, CONV)], axis=0
            ).astype(BF16)
            shift_buf[i] = shift
        else:
            shift = shift_buf[i]
        for part in parts:
            begin_at, size = part_at[part]
            source = ext[at : at + reach, begin_at : begin_at + size]
            moved = dot(shift, source, ((1,), (0,)))
            h = conv_bias[part] + taps[part][3:4] * source[HALO:].astype(F32)
            h = h + taps[part][2:3] * moved[:TILE]
            h = h + taps[part][1:2] * moved[TILE : 2 * TILE]
            h = h + taps[part][0:1] * moved[2 * TILE :]
            mixed[at : at + TILE, begin_at : begin_at + size] = silu_half(h).astype(BF16)

    loads[0].wait()
    loads[1].wait()
    for i in range(1, tiles):
        conv_tile(i, (0, 1))

    @pl.when(ctx > 0)
    def _():
        for i in range(3):
            halo_copy(i).wait_recv()

    conv_tile(0, (0, 1))

    state = jnp.zeros((STATE, width), F32)
    for c in range(blocks):
        at = c * BLOCK
        state_buf[c] = state
        x_tail = (mixed[at : at + BLOCK, :width].astype(F32) * tail_buf[at : at + BLOCK, :]).astype(
            BF16
        )
        summary = dot(mixed[at : at + BLOCK, width : width + STATE], x_tail, ((0,), (0,)))
        state = state * decay_rows[c] + summary
    end_buf[...] = state
    shard_decay = decay_rows[0]
    for c in range(1, blocks):
        shard_decay = shard_decay * decay_rows[c]

    chunk = STATE // CHUNKS

    def state_copy(i):
        at = pl.ds(i * chunk, chunk)
        return pltpu.make_async_remote_copy(
            src_ref=send_buf.at[at, :],
            dst_ref=recv_buf.at[at, :],
            send_sem=state_send.at[i],
            recv_sem=state_recv.at[i],
            device_id=right,
            device_id_type=pl.DeviceIdType.MESH,
        )

    @pl.when((ctx == 0) & not_last)
    def _():
        for i in range(CHUNKS):
            at = pl.ds(i * chunk, chunk)
            send_buf[at, :] = end_buf[at, :].astype(BF16)
            state_copy(i).start()

    def pass_on(turn, chunks):
        @pl.when(turn & not_last)
        def _():
            for i in chunks:
                at = pl.ds(i * chunk, chunk)
                state_copy(i).wait_recv()
                send_buf[at, :] = (
                    end_buf[at, :] + shard_decay * recv_buf[at, :].astype(F32)
                ).astype(BF16)
                state_copy(i).start()

    pace = CHUNKS // blocks

    entry_buf[...] = dot(split_rows(entry_rows, 2), spread2, ((0,), (0,)))
    loads[2].wait()
    loads[3].wait()
    gap_at = lax.broadcasted_iota(jnp.int32, (BLOCK, BLOCK), 0) - lax.broadcasted_iota(
        jnp.int32, (BLOCK, BLOCK), 1
    )
    for c in range(blocks):
        at = c * BLOCK
        for i in range(BLOCK // TILE):
            conv_tile(c * (BLOCK // TILE) + i, (2,))
        x_c = mixed[at : at + BLOCK, :width]
        b_c = mixed[at : at + BLOCK, width : width + STATE]
        c_c = mixed[at : at + BLOCK, width + STATE :]
        inner = dot(c_c, b_c, ((1,), (1,)))
        inner = jnp.where((gap_at >= 0) & (gap_at <= left[:, at : at + BLOCK]), inner, 0.0)
        x_heads = [x_c * (head_lane == h).astype(F32).astype(BF16) for h in range(heads)]
        for lo in range(0, BLOCK, TILE):
            hi = lo + TILE
            y = skip_row * x_c[lo:hi].astype(F32)
            for h in range(heads):
                r = c * heads + h
                gap = jnp.minimum(run_col[lo:hi, r : r + 1] - run[r : r + 1, :hi], 0.0)
                mix = jnp.exp2(gap) * inner[lo:hi, :hi] * step[h : h + 1, at : at + hi]
                y = y + dot(mix.astype(BF16), x_heads[h][:hi], ((1,), (0,)))
            y_buf[at + lo : at + hi, :] = y
        pass_on(ctx == 1, range(c * pace, (c + 1) * pace))
        if c >= 2:
            pass_on(ctx == 2, range((c - 2) * pace, (c - 1) * pace))

    pass_on(ctx == 2, range(max(0, blocks - 2) * pace, CHUNKS))
    pass_on(ctx >= 3, range(CHUNKS))
    for c in range(blocks):
        at = c * BLOCK
        gate_buf[at : at + BLOCK, :] = silu_half(z_buf[at : at + BLOCK, :].astype(F32) * 0.5)
        if c > 0:
            local = dot(
                mixed[at : at + BLOCK, width + STATE :], state_buf[c].astype(BF16), ((1,), (0,))
            )
            y_buf[at : at + BLOCK, :] += entry_buf[at : at + BLOCK, :] * local

    @pl.when((ctx > 0) & (ctx == n_ctx - 1))
    def _():
        for i in range(CHUNKS):
            state_copy(i).wait_recv()

    norm_row = nw_ref[...]
    entering = recv_buf[...]
    so_far = jnp.ones((1, width), F32)
    ones = jnp.ones((8, width), BF16)
    slot_row = lax.broadcasted_iota(jnp.int32, (tiles, TILE), 0)
    squares = jnp.zeros((tiles, TILE), F32)
    for c in range(blocks):
        at = c * BLOCK
        from_state = dot(mixed[at : at + BLOCK, width + STATE :], entering, ((1,), (0,)))
        y = y_buf[at : at + BLOCK, :] + entry_buf[at : at + BLOCK, :] * so_far * from_state
        so_far = so_far * decay_rows[c]
        gated = y * gate_buf[at : at + BLOCK, :]
        gated_ref[at : at + BLOCK, :] = gated * norm_row
        row = dot(ones, (gated * gated).astype(BF16), ((1,), (1,)))
        for i in range(BLOCK // TILE):
            squares = jnp.where(
                slot_row == c * (BLOCK // TILE) + i, row[0:1, i * TILE : (i + 1) * TILE], squares
            )
    sums[me] = squares

    def sums_copy(d):
        return pltpu.make_async_remote_copy(
            src_ref=sums.at[me],
            dst_ref=sums.at[me],
            send_sem=sums_send.at[d],
            recv_sem=sums_recv.at[d],
            device_id=(ctx, peers[d]),
            device_id_type=pl.DeviceIdType.MESH,
        )

    for d in range(n_head - 1):
        sums_copy(d).start()
    for d in range(n_head - 1):
        sums_copy(d).wait_recv()
    every = sums[0]
    for d in range(1, n_head):
        every = every + sums[d]
    scale_ref[...] = lax.rsqrt(every / (n_head * width) + NORM_FLOOR)

    for d in range(n_head - 1):
        sums_copy(d).wait_send()

    @pl.when(not_last)
    def _():
        for i in range(3):
            halo_copy(i).wait_send()
        for i in range(CHUNKS):
            state_copy(i).wait_send()


def scale_kernel(gated_ref, scale_ref, out_hbm, out_buf, out_sems):
    rows, width = gated_ref.shape
    stores = []
    for t in range(rows // TILE):
        at = pl.ds(t * TILE, TILE)
        column = jnp.transpose(jnp.broadcast_to(scale_ref[t : t + 1, :], (TILE, TILE)))
        column = jnp.concatenate([column] * (width // TILE), axis=1)
        out_buf[at, :] = (gated_ref[at, :] * column).astype(BF16)
        if t % 2 == 1:
            pair = pl.ds((t - 1) * TILE, 2 * TILE)
            store = pltpu.make_async_copy(
                out_buf.at[pair, :], out_hbm.at[pair, :], out_sems.at[t // 2]
            )
            store.start()
            stores.append(store)
    for store in stores:
        store.wait()


def shards(
    x_in,
    bc_in,
    z_in,
    dt_in,
    conv_x_w,
    conv_x_b,
    conv_bc_w,
    conv_bc_b,
    dt_bias,
    a_log,
    skip_gain,
    norm_w,
    doc_len,
):
    rows, width = x_in.shape
    n_ctx = lax.axis_size("context")
    n_head = lax.axis_size("head")
    blocks = rows // BLOCK
    tiles = rows // TILE
    anywhere = pl.BlockSpec(memory_space=pltpu.HBM)
    heads = dt_in.shape[0]
    docs = doc_len.shape[0]
    vmem = pl.BlockSpec(memory_space=pltpu.VMEM)
    dma = pltpu.SemaphoreType.DMA
    gated, scale = pl.pallas_call(
        functools.partial(layer_kernel, n_ctx, n_head),
        out_shape=(pltpu.VMEM((rows, width), F32), pltpu.VMEM((tiles, TILE), F32)),
        in_specs=[anywhere] * 13,
        out_specs=(vmem, vmem),
        scratch_shapes=[
            pltpu.VMEM((heads, rows), BF16),
            pltpu.VMEM((3, CONV, width), F32),
            pltpu.VMEM((3, 1, width), F32),
            pltpu.VMEM((1, width), F32),
            pltpu.SMEM((heads,), F32),
            pltpu.SMEM((heads,), F32),
            pltpu.SMEM((heads,), F32),
            pltpu.SMEM((docs,), jnp.int32),
            pltpu.VMEM((tiles, (CONV - 1) * TILE, TILE + HALO), BF16),
            pltpu.VMEM((rows + HALO, width + 2 * STATE), BF16),
            pltpu.VMEM((rows, width), BF16),
            pltpu.VMEM((rows, width + 2 * STATE), BF16),
            pltpu.VMEM((rows, width), F32),
            pltpu.VMEM((rows, width), F32),
            pltpu.VMEM((blocks, STATE, width), F32),
            pltpu.VMEM((STATE, width), F32),
            pltpu.VMEM((rows, width), F32),
            pltpu.VMEM((rows, width), F32),
            pltpu.VMEM((STATE, width), BF16),
            pltpu.VMEM((STATE, width), BF16),
            pltpu.VMEM((n_head, tiles, TILE), F32),
            dma((4,)),
            dma((12,)),
            dma((3,)),
            dma((3,)),
            dma((CHUNKS,)),
            dma((CHUNKS,)),
            dma((n_head - 1,)),
            dma((n_head - 1,)),
        ],
        compiler_params=pltpu.CompilerParams(
            collective_id=0, has_side_effects=True, vmem_limit_bytes=60 * 1024 * 1024
        ),
    )(
        x_in,
        bc_in,
        z_in,
        dt_in,
        conv_x_w,
        conv_x_b.reshape(1, -1),
        conv_bc_w,
        conv_bc_b.reshape(1, -1),
        dt_bias,
        a_log,
        skip_gain,
        norm_w.reshape(1, -1),
        doc_len,
    )
    return pl.pallas_call(
        scale_kernel,
        out_shape=jax.ShapeDtypeStruct((rows, width), BF16),
        in_specs=[vmem, vmem],
        out_specs=anywhere,
        scratch_shapes=[pltpu.VMEM((rows, width), BF16), dma((tiles // 2,))],
        compiler_params=pltpu.CompilerParams(vmem_limit_bytes=4 * 1024 * 1024),
    )(gated, scale)


def solution(mesh):
    return jax.shard_map(
        shards,
        mesh=mesh,
        in_specs=(
            P("context", "head"),
            P("context", None),
            P("context", "head"),
            P("head", "context"),
            P(None, "head"),
            P("head"),
            P(),
            P(),
            P("head"),
            P("head"),
            P("head"),
            P("head"),
            P(),
        ),
        out_specs=P("context", "head"),
        check_vma=False,
    )
```

```python
import functools
import math

import jax
import jax.numpy as jnp
from jax import lax
from jax.experimental import pallas as pl
from jax.experimental.pallas import tpu as pltpu
from jax.sharding import PartitionSpec as P

HEAD_DIM = 64
STATE = 256
GROUPS = 8
CONV = 4
BLOCK = 256
TILE = 128
HALO = 16
CHUNKS = 4
LOG2E = math.log2(math.e)
NORM_FLOOR = 1e-05
F32 = jnp.float32
BF16 = jnp.bfloat16


def dot(a, b, dims):
    return lax.dot_general(a, b, (dims, ((), ())), preferred_element_type=F32)


def silu_half(h):
    return h + h * jnp.tanh(h)


def split_rows(v, parts):
    pieces = []
    for _ in range(parts):
        piece = v.astype(BF16).astype(F32)
        pieces.append(piece)
        v = v - piece
    return jnp.concatenate(pieces, axis=0).astype(BF16)


def layer_kernel(
    n_ctx,
    n_head,
    x_hbm,
    bc_hbm,
    z_hbm,
    dt_hbm,
    xw_hbm,
    xb_hbm,
    bcw_hbm,
    bcb_hbm,
    dt_bias_hbm,
    a_log_hbm,
    skip_hbm,
    nw_hbm,
    doc_hbm,
    gated_ref,
    scale_ref,
    dt_ref,
    taps_buf,
    bias_buf,
    nw_ref,
    dt_bias,
    a_log,
    skip_gain,
    doc_len,
    shift_buf,
    ext,
    z_buf,
    mixed,
    tail_buf,
    entry_buf,
    state_buf,
    end_buf,
    y_buf,
    gate_buf,
    send_buf,
    recv_buf,
    sums,
    load_sems,
    small_sems,
    halo_send,
    halo_recv,
    state_send,
    state_recv,
    sums_send,
    sums_recv,
):
    rows = x_hbm.shape[0]
    width = x_hbm.shape[1]
    heads = dt_ref.shape[0]
    docs = doc_len.shape[0]
    blocks = rows // BLOCK
    tiles = rows // TILE
    ctx = lax.axis_index("context")
    me = lax.axis_index("head")
    per_group = n_head * heads // GROUPS
    group = me * heads // per_group
    b_at = pl.multiple_of(group * STATE, STATE)
    c_at = pl.multiple_of((GROUPS + group) * STATE, STATE)
    not_last = ctx < n_ctx - 1
    rounds = recv_buf.shape[0]

    barrier = pltpu.get_barrier_semaphore()

    @pl.when(ctx > 0)
    def _():
        pl.semaphore_signal(
            barrier, inc=1, device_id=(ctx - 1, me), device_id_type=pl.DeviceIdType.MESH
        )

    peers = [lax.rem(me + d, n_head) for d in range(1, n_head)]
    for peer in peers:
        pl.semaphore_signal(
            barrier, inc=1, device_id=(ctx, peer), device_id_type=pl.DeviceIdType.MESH
        )

    pairs = [
        (doc_hbm, doc_len),
        (dt_hbm, dt_ref),
        (dt_bias_hbm, dt_bias),
        (a_log_hbm, a_log),
        (skip_hbm, skip_gain),
        (xw_hbm, taps_buf.at[0]),
        (bcw_hbm.at[:, pl.ds(b_at, STATE)], taps_buf.at[1]),
        (bcw_hbm.at[:, pl.ds(c_at, STATE)], taps_buf.at[2]),
        (xb_hbm, bias_buf.at[0]),
        (bcb_hbm.at[:, pl.ds(b_at, STATE)], bias_buf.at[1]),
        (bcb_hbm.at[:, pl.ds(c_at, STATE)], bias_buf.at[2]),
        (nw_hbm, nw_ref),
    ]
    smalls = [
        pltpu.make_async_copy(src, dst, small_sems.at[i]) for i, (src, dst) in enumerate(pairs)
    ]
    for small in smalls:
        small.start()

    own = pl.ds(HALO, rows)
    loads = [
        pltpu.make_async_copy(x_hbm, ext.at[own, pl.ds(0, width)], load_sems.at[0]),
        pltpu.make_async_copy(
            bc_hbm.at[:, pl.ds(b_at, STATE)], ext.at[own, pl.ds(width, STATE)], load_sems.at[1]
        ),
        pltpu.make_async_copy(
            bc_hbm.at[:, pl.ds(c_at, STATE)],
            ext.at[own, pl.ds(width + STATE, STATE)],
            load_sems.at[2],
        ),
        pltpu.make_async_copy(z_hbm, z_buf, load_sems.at[3]),
    ]
    for load in loads:
        load.start()

    @pl.when(ctx == 0)
    def _():
        ext[pl.ds(0, HALO), :] = jnp.zeros((HALO, width + 2 * STATE), BF16)
        recv_buf[...] = jnp.zeros(recv_buf.shape, BF16)

    for small in smalls:
        small.wait()

    first = ctx * rows
    ends, begins, total = [], [], jnp.int32(0)
    for d in range(docs):
        begins.append(total)
        total = total + doc_len[d]
        ends.append(total)

    def tokens_left(pos):
        end = jnp.zeros_like(pos)
        for d in reversed(range(docs)):
            end = jnp.where(pos < ends[d], ends[d], end)
        return jnp.where(pos < 0, -1, end - 1 - pos)

    ext_lanes = rows + TILE
    left_ext = tokens_left(first - HALO + lax.broadcasted_iota(jnp.int32, (1, ext_lanes), 1))
    lane = lax.broadcasted_iota(jnp.int32, (1, rows), 1)
    pos = first + lane
    left = tokens_left(pos)
    begin = jnp.zeros_like(pos)
    for d in range(docs):
        begin = jnp.where(pos >= begins[d], begins[d], begin)
    lane_b = lax.rem(lane, BLOCK)
    alive = pos - begin > lane_b
    tail_same = left >= BLOCK - 1 - lane_b

    head_row = lax.broadcasted_iota(jnp.int32, (heads, rows), 0)
    bias_col = jnp.zeros((heads, rows), F32)
    alog_col = jnp.zeros((heads, rows), F32)
    for h in range(heads):
        bias_col = jnp.where(head_row == h, dt_bias[h], bias_col)
        alog_col = jnp.where(head_row == h, a_log[h], alog_col)
    raw = dt_ref[...].astype(F32) + bias_col
    step = jnp.maximum(raw, 0.0) + jnp.log1p(jnp.exp(-jnp.abs(raw)))
    log_decay = step * (jnp.exp(alog_col) * (-LOG2E))
    per_block = jnp.concatenate(
        [log_decay[:, c * BLOCK : (c + 1) * BLOCK] for c in range(blocks)], axis=0
    )
    upper = (
        lax.broadcasted_iota(jnp.int32, (BLOCK, BLOCK), 0)
        <= lax.broadcasted_iota(jnp.int32, (BLOCK, BLOCK), 1)
    )
    n_run = blocks * heads
    summed = dot(split_rows(per_block, 3), upper.astype(F32).astype(BF16), ((1,), (0,)))
    run = summed[:n_run] + summed[n_run : 2 * n_run] + summed[2 * n_run :]
    run_col = jnp.transpose(run)
    ends_run = run[:, BLOCK - 1 : BLOCK]
    running = jnp.concatenate([run[c * heads : (c + 1) * heads] for c in range(blocks)], axis=1)
    to_end = jnp.concatenate(
        [
            ends_run[c * heads : (c + 1) * heads] - run[c * heads : (c + 1) * heads]
            for c in range(blocks)
        ],
        axis=1,
    )
    tail_rows = jnp.where(tail_same, jnp.exp2(to_end), 0.0) * step
    entry_rows = jnp.where(alive, jnp.exp2(running), 0.0)

    spread = (
        lax.broadcasted_iota(jnp.int32, (heads, width), 0)
        == lax.broadcasted_iota(jnp.int32, (heads, width), 1) // HEAD_DIM
    ).astype(F32)
    spread2 = jnp.concatenate([spread, spread], axis=0).astype(BF16)
    tail_buf[...] = dot(split_rows(tail_rows, 2), spread2, ((0,), (0,)))

    decay_rows = []
    for c in range(blocks):
        at = c * BLOCK + BLOCK - 1
        decay_rows.append(jnp.sum(entry_rows[:, at : at + 1] * spread, axis=0, keepdims=True))
    skip_row = jnp.zeros((1, width), F32)
    head_lane = lax.broadcasted_iota(jnp.int32, (1, width), 1) // HEAD_DIM
    for h in range(heads):
        skip_row = jnp.where(head_lane == h, skip_gain[h], skip_row)

    pl.semaphore_wait(barrier, n_head - 1 + jnp.where(not_last, 1, 0))

    right = (jnp.minimum(ctx + 1, n_ctx - 1), me)
    last_rows = pl.ds(rows - HALO, HALO)
    halo_src = [
        x_hbm.at[last_rows, :],
        bc_hbm.at[last_rows, pl.ds(b_at, STATE)],
        bc_hbm.at[last_rows, pl.ds(c_at, STATE)],
    ]
    halo_at = [pl.ds(0, width), pl.ds(width, STATE), pl.ds(width + STATE, STATE)]

    def halo_copy(i):
        return pltpu.make_async_remote_copy(
            src_ref=halo_src[i],
            dst_ref=ext.at[pl.ds(0, HALO), halo_at[i]],
            send_sem=halo_send.at[i],
            recv_sem=halo_recv.at[i],
            device_id=right,
            device_id_type=pl.DeviceIdType.MESH,
        )

    @pl.when(not_last)
    def _():
        for i in range(3):
            halo_copy(i).start()

    reach = TILE + HALO
    offset = lax.broadcasted_iota(jnp.int32, (TILE, reach), 1) - lax.broadcasted_iota(
        jnp.int32, (TILE, reach), 0
    )
    bands = [jnp.where(offset == HALO - j, 1.0, 0.0).astype(F32) for j in range(1, CONV)]
    taps = [taps_buf[i] * 0.5 for i in range(3)]
    conv_bias = [bias_buf[i] * 0.5 for i in range(3)]
    part_at = [(0, width), (width, STATE), (width + STATE, STATE)]

    def conv_tile(i, parts):
        at = i * TILE
        if 0 in parts:
            ok = left_ext[:, at : at + reach]
            shift = jnp.concatenate(
                [jnp.where(ok >= j, bands[j - 1], 0.0) for j in range(1, CONV)], axis=0
            ).astype(BF16)
            shift_buf[i] = shift
        else:
            shift = shift_buf[i]
        for part in parts:
            begin_at, size = part_at[part]
            source = ext[at : at + reach, begin_at : begin_at + size]
            moved = dot(shift, source, ((1,), (0,)))
            h = conv_bias[part] + taps[part][3:4] * source[HALO:].astype(F32)
            h = h + taps[part][2:3] * moved[:TILE]
            h = h + taps[part][1:2] * moved[TILE : 2 * TILE]
            h = h + taps[part][0:1] * moved[2 * TILE :]
            mixed[at : at + TILE, begin_at : begin_at + size] = silu_half(h).astype(BF16)

    loads[0].wait()
    loads[1].wait()
    for i in range(1, tiles):
        conv_tile(i, (0, 1))

    @pl.when(ctx > 0)
    def _():
        for i in range(3):
            halo_copy(i).wait_recv()

    conv_tile(0, (0, 1))

    state = jnp.zeros((STATE, width), F32)
    for c in range(blocks):
        at = c * BLOCK
        state_buf[c] = state
        x_tail = (mixed[at : at + BLOCK, :width].astype(F32) * tail_buf[at : at + BLOCK, :]).astype(
            BF16
        )
        summary = dot(mixed[at : at + BLOCK, width : width + STATE], x_tail, ((0,), (0,)))
        state = state * decay_rows[c] + summary
    end_buf[...] = state
    shard_decay = decay_rows[0]
    for c in range(1, blocks):
        shard_decay = shard_decay * decay_rows[c]

    chunk = STATE // CHUNKS

    def state_copy(turn, i):
        at = pl.ds(i * chunk, chunk)
        return pltpu.make_async_remote_copy(
            src_ref=send_buf.at[turn, at, :],
            dst_ref=recv_buf.at[turn, at, :],
            send_sem=state_send.at[turn, i],
            recv_sem=state_recv.at[turn, i],
            device_id=right,
            device_id_type=pl.DeviceIdType.MESH,
        )

    @pl.when(not_last)
    def _():
        for i in range(CHUNKS):
            at = pl.ds(i * chunk, chunk)
            send_buf[0, at, :] = end_buf[at, :].astype(BF16)
            state_copy(0, i).start()

    def arrived(turn, chunks):
        @pl.when(ctx > 0)
        def _():
            for i in chunks:
                state_copy(turn, i).wait_recv()

    def pass_on(turn, chunks):
        for i in chunks:
            arrived(turn, [i])

            @pl.when(not_last)
            def _():
                at = pl.ds(i * chunk, chunk)
                send_buf[turn + 1, at, :] = (
                    end_buf[at, :] + shard_decay * recv_buf[turn, at, :].astype(F32)
                ).astype(BF16)
                state_copy(turn + 1, i).start()

    halves = [range(0, CHUNKS // 2), range(CHUNKS // 2, CHUNKS)]

    entry_buf[...] = dot(split_rows(entry_rows, 2), spread2, ((0,), (0,)))
    loads[2].wait()
    loads[3].wait()
    gap_at = lax.broadcasted_iota(jnp.int32, (BLOCK, BLOCK), 0) - lax.broadcasted_iota(
        jnp.int32, (BLOCK, BLOCK), 1
    )
    for c in range(blocks):
        at = c * BLOCK
        for i in range(BLOCK // TILE):
            conv_tile(c * (BLOCK // TILE) + i, (2,))
        x_c = mixed[at : at + BLOCK, :width]
        b_c = mixed[at : at + BLOCK, width : width + STATE]
        c_c = mixed[at : at + BLOCK, width + STATE :]
        inner = dot(c_c, b_c, ((1,), (1,)))
        inner = jnp.where((gap_at >= 0) & (gap_at <= left[:, at : at + BLOCK]), inner, 0.0)
        x_heads = [x_c * (head_lane == h).astype(F32).astype(BF16) for h in range(heads)]
        for lo in range(0, BLOCK, TILE):
            hi = lo + TILE
            y = skip_row * x_c[lo:hi].astype(F32)
            for h in range(heads):
                r = c * heads + h
                gap = jnp.minimum(run_col[lo:hi, r : r + 1] - run[r : r + 1, :hi], 0.0)
                mix = jnp.exp2(gap) * inner[lo:hi, :hi] * step[h : h + 1, at : at + hi]
                y = y + dot(mix.astype(BF16), x_heads[h][:hi], ((1,), (0,)))
            y_buf[at + lo : at + hi, :] = y
        if rounds > 1 and blocks - 3 <= c < blocks - 1:
            pass_on(0, halves[c - (blocks - 3)])

    for turn in range(1, rounds - 1):
        pass_on(turn, range(CHUNKS))
    for c in range(blocks):
        at = c * BLOCK
        gate_buf[at : at + BLOCK, :] = silu_half(z_buf[at : at + BLOCK, :].astype(F32) * 0.5)
        if c > 0:
            local = dot(
                mixed[at : at + BLOCK, width + STATE :], state_buf[c].astype(BF16), ((1,), (0,))
            )
            y_buf[at : at + BLOCK, :] += entry_buf[at : at + BLOCK, :] * local

    arrived(rounds - 1, range(CHUNKS))

    norm_row = nw_ref[...]
    entering = recv_buf[rounds - 1]
    so_far = jnp.ones((1, width), F32)
    ones = jnp.ones((8, width), BF16)
    slot_row = lax.broadcasted_iota(jnp.int32, (tiles, TILE), 0)
    squares = jnp.zeros((tiles, TILE), F32)
    for c in range(blocks):
        at = c * BLOCK
        from_state = dot(mixed[at : at + BLOCK, width + STATE :], entering, ((1,), (0,)))
        y = y_buf[at : at + BLOCK, :] + entry_buf[at : at + BLOCK, :] * so_far * from_state
        so_far = so_far * decay_rows[c]
        gated = y * gate_buf[at : at + BLOCK, :]
        gated_ref[at : at + BLOCK, :] = gated * norm_row
        row = dot(ones, (gated * gated).astype(BF16), ((1,), (1,)))
        for i in range(BLOCK // TILE):
            squares = jnp.where(
                slot_row == c * (BLOCK // TILE) + i, row[0:1, i * TILE : (i + 1) * TILE], squares
            )
    sums[me] = squares

    def sums_copy(d):
        return pltpu.make_async_remote_copy(
            src_ref=sums.at[me],
            dst_ref=sums.at[me],
            send_sem=sums_send.at[d],
            recv_sem=sums_recv.at[d],
            device_id=(ctx, peers[d]),
            device_id_type=pl.DeviceIdType.MESH,
        )

    for d in range(n_head - 1):
        sums_copy(d).start()
    for d in range(n_head - 1):
        sums_copy(d).wait_recv()
    every = sums[0]
    for d in range(1, n_head):
        every = every + sums[d]
    scale_ref[...] = lax.rsqrt(every / (n_head * width) + NORM_FLOOR)

    for d in range(n_head - 1):
        sums_copy(d).wait_send()

    @pl.when(not_last)
    def _():
        for i in range(3):
            halo_copy(i).wait_send()
        for turn in range(rounds):
            for i in range(CHUNKS):
                state_copy(turn, i).wait_send()


def scale_kernel(gated_ref, scale_ref, out_hbm, out_buf, out_sems):
    rows, width = gated_ref.shape
    stores = []
    for t in range(rows // TILE):
        at = pl.ds(t * TILE, TILE)
        column = jnp.transpose(jnp.broadcast_to(scale_ref[t : t + 1, :], (TILE, TILE)))
        column = jnp.concatenate([column] * (width // TILE), axis=1)
        out_buf[at, :] = (gated_ref[at, :] * column).astype(BF16)
        if t % 2 == 1:
            pair = pl.ds((t - 1) * TILE, 2 * TILE)
            store = pltpu.make_async_copy(
                out_buf.at[pair, :], out_hbm.at[pair, :], out_sems.at[t // 2]
            )
            store.start()
            stores.append(store)
    for store in stores:
        store.wait()


def shards(
    x_in,
    bc_in,
    z_in,
    dt_in,
    conv_x_w,
    conv_x_b,
    conv_bc_w,
    conv_bc_b,
    dt_bias,
    a_log,
    skip_gain,
    norm_w,
    doc_len,
):
    rows, width = x_in.shape
    n_ctx = lax.axis_size("context")
    n_head = lax.axis_size("head")
    rounds = max(1, n_ctx // 2)
    blocks = rows // BLOCK
    tiles = rows // TILE
    anywhere = pl.BlockSpec(memory_space=pltpu.HBM)
    heads = dt_in.shape[0]
    docs = doc_len.shape[0]
    vmem = pl.BlockSpec(memory_space=pltpu.VMEM)
    dma = pltpu.SemaphoreType.DMA
    gated, scale = pl.pallas_call(
        functools.partial(layer_kernel, n_ctx, n_head),
        out_shape=(pltpu.VMEM((rows, width), F32), pltpu.VMEM((tiles, TILE), F32)),
        in_specs=[anywhere] * 13,
        out_specs=(vmem, vmem),
        scratch_shapes=[
            pltpu.VMEM((heads, rows), BF16),
            pltpu.VMEM((3, CONV, width), F32),
            pltpu.VMEM((3, 1, width), F32),
            pltpu.VMEM((1, width), F32),
            pltpu.SMEM((heads,), F32),
            pltpu.SMEM((heads,), F32),
            pltpu.SMEM((heads,), F32),
            pltpu.SMEM((docs,), jnp.int32),
            pltpu.VMEM((tiles, (CONV - 1) * TILE, TILE + HALO), BF16),
            pltpu.VMEM((rows + HALO, width + 2 * STATE), BF16),
            pltpu.VMEM((rows, width), BF16),
            pltpu.VMEM((rows, width + 2 * STATE), BF16),
            pltpu.VMEM((rows, width), F32),
            pltpu.VMEM((rows, width), F32),
            pltpu.VMEM((blocks, STATE, width), F32),
            pltpu.VMEM((STATE, width), F32),
            pltpu.VMEM((rows, width), F32),
            pltpu.VMEM((rows, width), F32),
            pltpu.VMEM((rounds, STATE, width), BF16),
            pltpu.VMEM((rounds, STATE, width), BF16),
            pltpu.VMEM((n_head, tiles, TILE), F32),
            dma((4,)),
            dma((12,)),
            dma((3,)),
            dma((3,)),
            dma((rounds, CHUNKS)),
            dma((rounds, CHUNKS)),
            dma((n_head - 1,)),
            dma((n_head - 1,)),
        ],
        compiler_params=pltpu.CompilerParams(
            collective_id=0, has_side_effects=True, vmem_limit_bytes=60 * 1024 * 1024
        ),
    )(
        x_in,
        bc_in,
        z_in,
        dt_in,
        conv_x_w,
        conv_x_b.reshape(1, -1),
        conv_bc_w,
        conv_bc_b.reshape(1, -1),
        dt_bias,
        a_log,
        skip_gain,
        norm_w.reshape(1, -1),
        doc_len,
    )
    return pl.pallas_call(
        scale_kernel,
        out_shape=jax.ShapeDtypeStruct((rows, width), BF16),
        in_specs=[vmem, vmem],
        out_specs=anywhere,
        scratch_shapes=[pltpu.VMEM((rows, width), BF16), dma((tiles // 2,))],
        compiler_params=pltpu.CompilerParams(vmem_limit_bytes=4 * 1024 * 1024),
    )(gated, scale)


def solution(mesh):
    return jax.shard_map(
        shards,
        mesh=mesh,
        in_specs=(
            P("context", "head"),
            P("context", None),
            P("context", "head"),
            P("head", "context"),
            P(None, "head"),
            P("head"),
            P(),
            P(),
            P("head"),
            P("head"),
            P("head"),
            P("head"),
            P(),
        ),
        out_specs=P("context", "head"),
        check_vma=False,
    )
```
